512 devices in a mesh: tm: 64 (over z, y), panel: 8 (over x, core).
Axes of the slice: x: 4, y: 8, z: 8, core: 2. Of those that a mesh axis runs over, the one named last changes fastest.
Arguments:
- factor_inverse: float32 [64, 768, 768], P('tm', None, 'panel'), may hold values from -1 to 1, as said below
- coupling: float32 [64, 768, 768], P('tm', None, 'panel'), may hold values from -1 to 1
- sigma_after: float32 [768, 768], replicated, may hold values from -1 to 3, as said below
Outputs:
- marginal_cov: float32 [64, 768, 768], P('tm', None, 'panel')
- propagator: bfloat16 [64, 768, 768], P('tm', None, 'panel')
The draws below stay inside these ranges and needn't reach their ends.
Inputs may be any that keep to these rules, and one draw needn't show every extreme that they name: `factor_inverse`: factor_inverse_t is lower triangular with a positive diagonal. sigma_after is symmetric.
All inputs are finite; a program needn't handle non-finite values.
Results may differ from the reference program's by a relative error of at most 0.007.
The reference program's roundings to bfloat16 on the way count: a program that leaves them out, or rounds other values in their place, can miss the bound.
Values may be sent and summed in bfloat16 or wider, within the bound.
A program may use at most 64 MiB of HBM per device.

```python
import math
import jax
import jax.numpy as jnp
from jax import lax

NB = 768
TIME_BLOCKS = 64


def draw_factor_inverse(key, part):
    key = jax.random.fold_in(key, 11)
    random_key_list = jax.random.split(key, 2)
    diagonal = jnp.exp(jax.random.uniform(random_key_list[0], (TIME_BLOCKS, NB), jnp.float32, math.log(0.1), math.log(0.3)))
    spread = jax.random.normal(random_key_list[1], (TIME_BLOCKS, NB, NB), jnp.float32)
    lower_mask = jnp.tril(jnp.ones((NB, NB), jnp.float32), -1)
    identity = jnp.eye(NB, dtype=jnp.float32)
    body_part = spread * (0.1 / math.sqrt(NB)) * lower_mask + identity * diagonal[:, None, :]
    return body_part


def draw_coupling(key, part):
    key = jax.random.fold_in(key, 23)
    random_key_list = jax.random.split(key, 6)
    slow_flag = jax.random.randint(random_key_list[0], (NB,), 0, 2) == 1
    noise = jax.random.normal(random_key_list[1], (TIME_BLOCKS, NB, NB), jnp.float32)
    slow_rate = jnp.exp(jax.random.uniform(random_key_list[2], (NB,), jnp.float32, math.log(0.5), math.log(1.2))) / TIME_BLOCKS
    fast_rate = jnp.exp(jax.random.uniform(random_key_list[3], (NB,), jnp.float32, math.log(0.1), math.log(0.6)))
    rate = jnp.where(slow_flag, slow_rate, fast_rate)
    block_factor = jnp.exp(jax.random.uniform(random_key_list[4], (TIME_BLOCKS, 1), jnp.float32, math.log(0.7), math.log(1.4)))
    damping_factor = 1.0 - rate[None, :] * block_factor
    spike_block_count = jax.random.randint(random_key_list[5], (3,), 0, TIME_BLOCKS)
    spike_triggered = jnp.any(jnp.arange(TIME_BLOCKS)[:, None] == spike_block_count[None, :], axis=1)
    damping_factor = damping_factor * jnp.where(spike_triggered, 0.75, 1.0)[:, None]
    identity = jnp.eye(NB, dtype=jnp.float32)
    return noise * (0.2 / math.sqrt(NB)) * (1.0 - identity) + identity * damping_factor[:, None, :]


def draw_sigma_after(key, part):
    key = jax.random.fold_in(key, 37)
    random_key_list = jax.random.split(key, 2)
    diagonal = jax.random.uniform(random_key_list[0], (NB,), jnp.float32, 0.5, 1.5)
    noise = jax.random.normal(random_key_list[1], (NB, NB), jnp.float32)
    symmetrized_matrix = (noise + noise.T) * (0.2 / math.sqrt(NB))
    identity = jnp.eye(NB, dtype=jnp.float32)
    return symmetrized_matrix * (1.0 - identity) + identity * diagonal[None, :]


def setup_inputs(seed: int = 0) -> dict:
    arg_keys = jax.random.split(jax.random.key(seed), 4)
    return {
        "factor_inverse": draw_factor_inverse(jax.random.fold_in(arg_keys[3], 71), 0),
        "coupling": draw_coupling(jax.random.fold_in(arg_keys[3], 71), 0),
        "sigma_after": draw_sigma_after(jax.random.fold_in(arg_keys[3], 71), 0),
    }


def reference(factor_inverse, coupling, sigma_after):
    highest = lax.Precision.HIGHEST
    rounded = coupling.astype(jnp.bfloat16)
    covariance = jnp.einsum("tki,tkj->tij", factor_inverse, factor_inverse, precision=highest)
    last_block = rounded[-1].astype(jnp.float32)
    folded = jnp.dot(last_block.T, jnp.dot(sigma_after, last_block, precision=highest), precision=highest)
    covariance = covariance.at[-1].add(folded)
    composite = rounded
    distance = 1
    while distance < TIME_BLOCKS:
        partner_bf = lax.optimization_barrier(covariance[distance:].astype(jnp.bfloat16))
        partner_cov = partner_bf.astype(jnp.float32)
        own_comp = composite[:-distance].astype(jnp.float32)
        middle_bf = jnp.einsum("tij,tjk->tik", partner_cov, own_comp, precision=highest).astype(jnp.bfloat16)
        middle = lax.optimization_barrier(middle_bf).astype(jnp.float32)
        update = jnp.einsum("tji,tjk->tik", own_comp, middle, precision=highest)
        covariance = jnp.concatenate([covariance[:-distance] + update, covariance[-distance:]], axis=0)
        partner_comp = composite[distance:].astype(jnp.float32)
        extended_complement = jnp.einsum("tij,tjk->tik", partner_comp, own_comp, precision=highest).astype(jnp.bfloat16)
        composite = jnp.concatenate([extended_complement, composite[-distance:]], axis=0)
        distance = distance * 2
    return covariance, composite
```

```python
import functools

import jax
import jax.numpy as jnp
from jax import lax
from jax.experimental import pallas as pl
from jax.experimental.pallas import tpu as pltpu
from jax.sharding import PartitionSpec as P

MESH = pl.DeviceIdType.MESH
F32 = jnp.float32
BF16 = jnp.bfloat16


def dot(a, b):
    return jnp.dot(a, b, preferred_element_type=F32)


def dot_nt(a, b):
    return lax.dot_general(a, b, (((1,), (1,)), ((), ())), preferred_element_type=F32)


def split(a):
    high = a.astype(BF16)
    return high, (a - high.astype(F32)).astype(BF16)


def kernel(
    steps, chips, rounds,
    factor_ref, coupling_ref, sigma_ref, cov_out, prop_out,
    comp, comp_t, fac_t, own_cov, cov_send, comp_recv, cov_recv, blocks, gathered, sigma_buf,
    g_send, g_recv, t_send, t_recv, a_send, a_recv, sigma_sem,
):
    width, n = own_cov.shape
    panels = 2 * chips
    t = lax.axis_index("tm")
    p = lax.axis_index("panel")
    x, c = lax.div(p, 2), lax.rem(p, 2)
    sibling = 2 * x + 1 - c
    last = t == steps - 1
    pending = []

    def has_source(r):
        return t + (1 << r) < steps

    def has_target(r):
        return t - (1 << r) >= 0

    def rows(q):
        return pl.ds(pl.multiple_of(q * width, 32), width)

    def away(dx, core):
        return 2 * lax.rem(x + chips + dx, chips) + core

    def send(cond, make):
        make().start()
        pending.append((cond, make))

    def copy(src, dst, s, r, tm, panel):
        return pltpu.make_async_remote_copy(
            src_ref=src, dst_ref=dst, send_sem=s, recv_sem=r, device_id=(tm, panel), device_id_type=MESH
        )

    def gather_copy(k, buf, q, i, to):
        return copy(buf().at[rows(q)], buf().at[rows(q)], g_send.at[k, i], g_recv.at[k, i], t, to)

    def start_gather(k, buf, cond=None):
        for dx in (2, 1, 3)[: chips - 1] if chips > 2 else (1,):
            send(cond, lambda dx=dx: gather_copy(k, buf, p, dx - 1, away(dx, c)))
        send(cond, lambda: gather_copy(k, buf, p, 3, sibling))

    def finish_gather(k, buf, cond=None):
        for dx in (1, 3, 2)[: chips - 1] if chips > 2 else (1,):
            gather_copy(k, buf, away(-dx, c), dx - 1, sibling).wait_recv()
            send(cond, lambda dx=dx: gather_copy(k, buf, away(-dx, c), 3 + dx, sibling))
        gather_copy(k, buf, sibling, 3, sibling).wait_recv()
        for dx in (1, 3, 2)[: chips - 1] if chips > 2 else (1,):
            gather_copy(k, buf, away(-dx, 1 - c), 3 + dx, sibling).wait_recv()

    def exchange_copy(k, src, dst, j, to):
        return copy(blocks.at[k, src], gathered.at[k, rows(dst)], a_send.at[k, j - 1], a_recv.at[k, j - 1], t, to)

    def start_exchange(k, panel, cond=None):
        wide = jnp.concatenate([panel, panel[:, :128]], axis=1)
        for q in range(panels):
            blocks[k, q] = wide[:, q * width : q * width + 128]
        for j in range(1, panels):
            q = lambda j=j: lax.rem(p + j, panels)
            send(cond, lambda j=j, q=q: exchange_copy(k, q(), p, j, q()))
        gathered[k, rows(p)] = blocks[k, p]

    def finish_exchange(k):
        for j in range(1, panels):
            q = lax.rem(p + panels - j, panels)
            exchange_copy(k, q, q, j, q).wait_recv()

    def comp_copy(r, to):
        return copy(comp.at[r, rows(p)], comp_recv.at[r], t_send.at[r, 0], t_recv.at[r, 0], to, p)

    def cov_copy(r, to):
        return copy(cov_send.at[r], cov_recv.at[r], t_send.at[r, 1], t_recv.at[r, 1], to, p)

    def send_comp(r):
        @pl.when(has_target(r))
        def _():
            send(lambda: has_target(r), lambda: comp_copy(r, t - (1 << r)))

    def send_cov(r):
        cov_send[r] = own_cov[...].astype(BF16)

        @pl.when(has_target(r))
        def _():
            send(lambda: has_target(r), lambda: cov_copy(r, t - (1 << r)))

    @pl.when(last)
    def _():
        pltpu.make_async_copy(sigma_ref, sigma_buf, sigma_sem).start()

    barrier = pltpu.get_barrier_semaphore()
    for j in range(1, panels):
        pl.semaphore_signal(barrier, 1, device_id=(t, lax.rem(p + j, panels)), device_id_type=MESH)
    for r in range(rounds):
        @pl.when(has_target(r))
        def _():
            pl.semaphore_signal(barrier, 1, device_id=(t - (1 << r), p), device_id_type=MESH)

        @pl.when(has_source(r))
        def _():
            pl.semaphore_signal(barrier, 1, device_id=(t + (1 << r), p), device_id_type=MESH)

    comp_t[rows(p)] = coupling_ref[...].T.astype(BF16)
    fac_high, fac_low = split(factor_ref[...].T)
    fac_t[rows(p)] = fac_high

    peers = panels - 1
    for r in range(rounds):
        peers += has_target(r).astype(jnp.int32) + has_source(r).astype(jnp.int32)
    pl.semaphore_wait(barrier, peers)

    start_gather(rounds, lambda: comp_t)
    start_gather(0, lambda: fac_t)
    finish_gather(rounds, lambda: comp_t)
    for j in range(n // 128):
        comp[0, :, 128 * j : 128 * (j + 1)] = comp_t[128 * j : 128 * (j + 1), :].T
    send_comp(0)
    finish_gather(0, lambda: fac_t)
    own_cov[...] = dot_nt(fac_high, fac_t[...]) + dot_nt(fac_low, fac_t[...])

    @pl.when(last)
    def _():
        pltpu.make_async_copy(sigma_ref, sigma_buf, sigma_sem).wait()
        sig_high, sig_low = split(sigma_buf[...])
        own = comp_t[rows(p)]
        w_high, w_low = split(dot(own, sig_high) + dot(own, sig_low))
        own_cov[...] += dot(w_high, comp[0]) + dot(w_low, comp[0])

    send_cov(0)

    for r in range(rounds):
        active = has_source(r)
        more = r + 1 < rounds
        if r:
            @pl.when(active)
            def _():
                finish_gather(r, lambda r=r: comp.at[r], lambda r=r: has_source(r))

        if more:
            @pl.when(active)
            def _():
                comp_copy(r, t).wait_recv()
                comp[r + 1, rows(p)] = dot(comp_recv[r], comp[r]).astype(BF16)

            @pl.when(jnp.logical_not(active))
            def _():
                comp[r + 1, rows(p)] = comp[r, rows(p)]

            send_comp(r + 1)

            @pl.when(has_source(r + 1))
            def _():
                start_gather(r + 1, lambda r=r: comp.at[r + 1], lambda r=r: has_source(r + 1))
        else:
            @pl.when(active)
            def _():
                comp_copy(r, t).wait_recv()
                start_exchange(rounds, dot(comp_recv[r], comp[r]).astype(BF16), lambda r=r: has_source(r))

            @pl.when(jnp.logical_not(active))
            def _():
                start_exchange(rounds, comp[r, rows(p)], lambda r=r: jnp.logical_not(has_source(r)))

        @pl.when(active)
        def _():
            cov_copy(r, t).wait_recv()
            start_exchange(r, dot(cov_recv[r], comp[r]).astype(BF16), lambda r=r: has_source(r))
            finish_exchange(r)
            middle_t = gathered[r].T[:width]
            own_cov[...] += dot(middle_t, comp[r])

        if more:
            send_cov(r + 1)

    cov_out[...] = own_cov[...].T
    finish_exchange(rounds)
    prop_out[...] = gathered[rounds][:, :width]

    for cond, make in pending:
        if cond is None:
            make().wait_send()
        else:
            pl.when(cond())(lambda make=make: make().wait_send())


def shards(factor_inverse, coupling, sigma_after):
    steps, panels = lax.axis_size("tm"), lax.axis_size("panel")
    n, width = factor_inverse.shape[1:]
    rounds = (steps - 1).bit_length()
    chips = panels // 2
    vmem = pl.BlockSpec(memory_space=pltpu.VMEM)
    cov, prop = pl.pallas_call(
        functools.partial(kernel, steps, chips, rounds),
        out_shape=(
            jax.ShapeDtypeStruct((n, width), F32),
            jax.ShapeDtypeStruct((n, width), BF16),
        ),
        in_specs=[vmem, vmem, pl.BlockSpec(memory_space=pl.ANY)],
        out_specs=(vmem, vmem),
        scratch_shapes=[
            pltpu.VMEM((rounds, n, n), BF16),
            pltpu.VMEM((n, n), BF16),
            pltpu.VMEM((n, n), BF16),
            pltpu.VMEM((width, n), F32),
            pltpu.VMEM((rounds, width, n), BF16),
            pltpu.VMEM((rounds, width, n), BF16),
            pltpu.VMEM((rounds, width, n), BF16),
            pltpu.VMEM((rounds + 1, panels, width, 128), BF16),
            pltpu.VMEM((rounds + 1, n, 128), BF16),
            pltpu.VMEM((n, n), F32),
            pltpu.SemaphoreType.DMA((rounds + 1, 7)),
            pltpu.SemaphoreType.DMA((rounds + 1, 7)),
            pltpu.SemaphoreType.DMA((rounds, 2)),
            pltpu.SemaphoreType.DMA((rounds, 2)),
            pltpu.SemaphoreType.DMA((rounds + 1, panels - 1)),
            pltpu.SemaphoreType.DMA((rounds + 1, panels - 1)),
            pltpu.SemaphoreType.DMA,
        ],
        compiler_params=pltpu.CompilerParams(
            collective_id=0, has_side_effects=True, vmem_limit_bytes=48 << 20
        ),
        name="scan",
    )(factor_inverse[0], coupling[0], sigma_after)
    return cov[None], prop[None]


def solution(mesh):
    placed = (P("tm", None, "panel"), P("tm", None, "panel"), P())
    return jax.shard_map(
        shards,
        mesh=mesh,
        in_specs=placed,
        out_specs=(P("tm", None, "panel"), P("tm", None, "panel")),
        check_vma=False,
    )
```

```python
import functools

import jax
import jax.numpy as jnp
from jax import lax
from jax.experimental import pallas as pl
from jax.experimental.pallas import tpu as pltpu
from jax.sharding import PartitionSpec as P

MESH = pl.DeviceIdType.MESH
F32 = jnp.float32
BF16 = jnp.bfloat16


def dot(a, b):
    return jnp.dot(a, b, preferred_element_type=F32)


def dot_nt(a, b):
    return lax.dot_general(a, b, (((1,), (1,)), ((), ())), preferred_element_type=F32)


def split(a):
    high = a.astype(BF16)
    return high, (a - high.astype(F32)).astype(BF16)


def kernel(
    steps, chips, rounds,
    factor_ref, coupling_ref, sigma_ref, cov_out, prop_out,
    comp, comp_t, fac_t, coupling_buf, factor_buf, own_cov, cov_send, comp_recv, cov_recv, blocks, gathered, sigma_buf,
    g_send, g_recv, t_send, t_recv, a_send, a_recv, load_sem,
):
    width, n = own_cov.shape
    panels = 2 * chips
    t = lax.axis_index("tm")
    p = lax.axis_index("panel")
    x, c = lax.div(p, 2), lax.rem(p, 2)
    sibling = 2 * x + 1 - c
    last = t == steps - 1
    pending = []

    def has_source(r):
        return t + (1 << r) < steps

    def has_target(r):
        return t - (1 << r) >= 0

    def rows(q):
        return pl.ds(pl.multiple_of(q * width, 32), width)

    def away(dx, core):
        return 2 * lax.rem(x + chips + dx, chips) + core

    def send(cond, make):
        make().start()
        pending.append((cond, make))

    def copy(src, dst, s, r, tm, panel):
        return pltpu.make_async_remote_copy(
            src_ref=src, dst_ref=dst, send_sem=s, recv_sem=r, device_id=(tm, panel), device_id_type=MESH
        )

    def gather_copy(k, buf, q, i, to):
        return copy(buf().at[rows(q)], buf().at[rows(q)], g_send.at[k, i], g_recv.at[k, i], t, to)

    def start_gather(k, buf, cond=None):
        for dx in (2, 1, 3)[: chips - 1] if chips > 2 else (1,):
            send(cond, lambda dx=dx: gather_copy(k, buf, p, dx - 1, away(dx, c)))
        send(cond, lambda: gather_copy(k, buf, p, 3, sibling))

    def finish_gather(k, buf, cond=None):
        for dx in (1, 3, 2)[: chips - 1] if chips > 2 else (1,):
            gather_copy(k, buf, away(-dx, c), dx - 1, sibling).wait_recv()
            send(cond, lambda dx=dx: gather_copy(k, buf, away(-dx, c), 3 + dx, sibling))
        gather_copy(k, buf, sibling, 3, sibling).wait_recv()
        for dx in (1, 3, 2)[: chips - 1] if chips > 2 else (1,):
            gather_copy(k, buf, away(-dx, 1 - c), 3 + dx, sibling).wait_recv()

    def exchange_copy(k, src, dst, j, to):
        return copy(blocks.at[k, src], gathered.at[k, rows(dst)], a_send.at[k, j - 1], a_recv.at[k, j - 1], t, to)

    def start_exchange(k, panel, cond=None):
        wide = jnp.concatenate([panel, panel[:, :128]], axis=1)
        for q in range(panels):
            blocks[k, q] = wide[:, q * width : q * width + 128]
        for j in sorted(range(1, panels), key=lambda j: abs(j - chips)):
            q = lambda j=j: lax.rem(p + j, panels)
            send(cond, lambda j=j, q=q: exchange_copy(k, q(), p, j, q()))
        gathered[k, rows(p)] = blocks[k, p]

    def finish_exchange(k):
        for j in range(1, panels):
            q = lax.rem(p + panels - j, panels)
            exchange_copy(k, q, q, j, q).wait_recv()

    def comp_copy(r, to):
        return copy(comp.at[r, rows(p)], comp_recv.at[r], t_send.at[r, 0], t_recv.at[r, 0], to, p)

    def cov_copy(r, to):
        return copy(cov_send.at[r], cov_recv.at[r], t_send.at[r, 1], t_recv.at[r, 1], to, p)

    def send_comp(r):
        @pl.when(has_target(r))
        def _():
            send(lambda: has_target(r), lambda: comp_copy(r, t - (1 << r)))

    def send_cov(r):
        cov_send[r] = own_cov[...].astype(BF16)

        @pl.when(has_target(r))
        def _():
            send(lambda: has_target(r), lambda: cov_copy(r, t - (1 << r)))

    loads = [
        pltpu.make_async_copy(coupling_ref, coupling_buf, load_sem.at[0]),
        pltpu.make_async_copy(factor_ref, factor_buf, load_sem.at[1]),
    ]
    for load in loads:
        load.start()

    @pl.when(last)
    def _():
        pltpu.make_async_copy(sigma_ref, sigma_buf, load_sem.at[2]).start()

    barrier = pltpu.get_barrier_semaphore()
    for j in range(1, panels):
        pl.semaphore_signal(barrier, 1, device_id=(t, lax.rem(p + j, panels)), device_id_type=MESH)
    for r in range(rounds):
        @pl.when(has_target(r))
        def _():
            pl.semaphore_signal(barrier, 1, device_id=(t - (1 << r), p), device_id_type=MESH)

        @pl.when(has_source(r))
        def _():
            pl.semaphore_signal(barrier, 1, device_id=(t + (1 << r), p), device_id_type=MESH)

    loads[0].wait()
    comp_t[rows(p)] = coupling_buf[...].astype(BF16)
    loads[1].wait()
    fac_high, fac_low = split(factor_buf[...])
    fac_t[rows(p)] = fac_high

    peers = panels - 1
    for r in range(rounds):
        peers += has_target(r).astype(jnp.int32) + has_source(r).astype(jnp.int32)
    pl.semaphore_wait(barrier, peers)

    start_gather(rounds, lambda: comp_t)
    start_gather(0, lambda: fac_t)
    finish_gather(rounds, lambda: comp_t)
    for j in range(n // 128):
        comp[0, :, 128 * j : 128 * (j + 1)] = comp_t[128 * j : 128 * (j + 1), :].T
    send_comp(0)
    finish_gather(0, lambda: fac_t)
    own_cov[...] = dot_nt(fac_high, fac_t[...]) + dot_nt(fac_low, fac_t[...])

    @pl.when(last)
    def _():
        pltpu.make_async_copy(sigma_ref, sigma_buf, load_sem.at[2]).wait()
        sig_high, sig_low = split(sigma_buf[...])
        own = comp_t[rows(p)]
        w_high, w_low = split(dot(own, sig_high) + dot(own, sig_low))
        own_cov[...] += dot(w_high, comp[0]) + dot(w_low, comp[0])

    send_cov(0)

    for r in range(rounds):
        active = has_source(r)
        more = r + 1 < rounds
        if r:
            @pl.when(active)
            def _():
                finish_gather(r, lambda r=r: comp.at[r], lambda r=r: has_source(r))

        if more:
            @pl.when(active)
            def _():
                comp_copy(r, t).wait_recv()
                comp[r + 1, rows(p)] = dot(comp_recv[r], comp[r]).astype(BF16)

            @pl.when(jnp.logical_not(active))
            def _():
                comp[r + 1, rows(p)] = comp[r, rows(p)]

            send_comp(r + 1)

            @pl.when(has_source(r + 1))
            def _():
                start_gather(r + 1, lambda r=r: comp.at[r + 1], lambda r=r: has_source(r + 1))
        else:
            @pl.when(active)
            def _():
                comp_copy(r, t).wait_recv()
                start_exchange(rounds, dot(comp_recv[r], comp[r]).astype(BF16), lambda r=r: has_source(r))

            @pl.when(jnp.logical_not(active))
            def _():
                start_exchange(rounds, comp[r, rows(p)], lambda r=r: jnp.logical_not(has_source(r)))

        @pl.when(active)
        def _():
            cov_copy(r, t).wait_recv()
            start_exchange(r, dot(cov_recv[r], comp[r]).astype(BF16), lambda r=r: has_source(r))
            finish_exchange(r)
            middle_t = gathered[r].T[:width]
            own_cov[...] += dot(middle_t, comp[r])

        if more:
            send_cov(r + 1)

    cov_out[...] = own_cov[...]
    finish_exchange(rounds)
    prop_out[...] = gathered[rounds].T[:width]

    for cond, make in pending:
        if cond is None:
            make().wait_send()
        else:
            pl.when(cond())(lambda make=make: make().wait_send())


def shards(factor_inverse, coupling, sigma_after):
    steps, panels = lax.axis_size("tm"), lax.axis_size("panel")
    n, width = factor_inverse.shape[1:]
    rounds = (steps - 1).bit_length()
    chips = panels // 2
    vmem = pl.BlockSpec(memory_space=pltpu.VMEM)
    cov, prop = pl.pallas_call(
        functools.partial(kernel, steps, chips, rounds),
        out_shape=(
            jax.ShapeDtypeStruct((width, n), F32),
            jax.ShapeDtypeStruct((width, n), BF16),
        ),
        in_specs=[pl.BlockSpec(memory_space=pl.ANY)] * 3,
        out_specs=(vmem, vmem),
        scratch_shapes=[
            pltpu.VMEM((rounds, n, n), BF16),
            pltpu.VMEM((n, n), BF16),
            pltpu.VMEM((n, n), BF16),
            pltpu.VMEM((width, n), F32),
            pltpu.VMEM((width, n), F32),
            pltpu.VMEM((width, n), F32),
            pltpu.VMEM((rounds, width, n), BF16),
            pltpu.VMEM((rounds, width, n), BF16),
            pltpu.VMEM((rounds, width, n), BF16),
            pltpu.VMEM((rounds + 1, panels, width, 128), BF16),
            pltpu.VMEM((rounds + 1, n, 128), BF16),
            pltpu.VMEM((n, n), F32),
            pltpu.SemaphoreType.DMA((rounds + 1, 7)),
            pltpu.SemaphoreType.DMA((rounds + 1, 7)),
            pltpu.SemaphoreType.DMA((rounds, 2)),
            pltpu.SemaphoreType.DMA((rounds, 2)),
            pltpu.SemaphoreType.DMA((rounds + 1, panels - 1)),
            pltpu.SemaphoreType.DMA((rounds + 1, panels - 1)),
            pltpu.SemaphoreType.DMA((3,)),
        ],
        compiler_params=pltpu.CompilerParams(
            collective_id=0, has_side_effects=True, vmem_limit_bytes=60 << 20
        ),
        name="scan",
    )(factor_inverse[0].T, coupling[0].T, sigma_after)
    return cov.T[None], prop.T[None]


def solution(mesh):
    placed = (P("tm", None, "panel"), P("tm", None, "panel"), P())
    return jax.shard_map(
        shards,
        mesh=mesh,
        in_specs=placed,
        out_specs=(P("tm", None, "panel"), P("tm", None, "panel")),
        check_vma=False,
    )
```

```python
import functools

import jax
import jax.numpy as jnp
from jax import lax
from jax.experimental import pallas as pl
from jax.experimental.pallas import tpu as pltpu
from jax.sharding import PartitionSpec as P

MESH = pl.DeviceIdType.MESH
F32 = jnp.float32
BF16 = jnp.bfloat16


def dot(a, b):
    return jnp.dot(a, b, preferred_element_type=F32)


def dot_nt(a, b):
    return lax.dot_general(a, b, (((1,), (1,)), ((), ())), preferred_element_type=F32)


def split(a):
    high = a.astype(BF16)
    return high, (a - high.astype(F32)).astype(BF16)


def kernel(
    steps, chips, rounds,
    factor_ref, coupling_ref, sigma_ref, cov_out, prop_out,
    comp, comp_t, fac_t, coupling_buf, factor_buf, own_cov, cov_send, comp_recv, cov_recv, blocks, gathered, sigma_buf,
    g_send, g_recv, t_send, t_recv, a_send, a_recv, load_sem,
):
    width, n = own_cov.shape
    panels = 2 * chips
    t = lax.axis_index("tm")
    p = lax.axis_index("panel")
    x, c = lax.div(p, 2), lax.rem(p, 2)
    sibling = 2 * x + 1 - c
    last = t == steps - 1
    pending = []

    def has_source(r):
        return t + (1 << r) < steps

    def has_target(r):
        return t - (1 << r) >= 0

    def rows(q):
        return pl.ds(pl.multiple_of(q * width, 32), width)

    def away(dx, core):
        return 2 * lax.rem(x + chips + dx, chips) + core

    def send(cond, make):
        make().start()
        pending.append((cond, make))

    def copy(src, dst, s, r, tm, panel):
        return pltpu.make_async_remote_copy(
            src_ref=src, dst_ref=dst, send_sem=s, recv_sem=r, device_id=(tm, panel), device_id_type=MESH
        )

    def gather_copy(k, buf, q, i, to):
        return copy(buf().at[rows(q)], buf().at[rows(q)], g_send.at[k, i], g_recv.at[k, i], t, to)

    def start_gather(k, buf, cond=None):
        for dx in (2, 1, 3)[: chips - 1] if chips > 2 else (1,):
            send(cond, lambda dx=dx: gather_copy(k, buf, p, dx - 1, away(dx, c)))
        send(cond, lambda: gather_copy(k, buf, p, 3, sibling))

    def finish_gather(k, buf, cond=None):
        for dx in (1, 3, 2)[: chips - 1] if chips > 2 else (1,):
            gather_copy(k, buf, away(-dx, c), dx - 1, sibling).wait_recv()
            send(cond, lambda dx=dx: gather_copy(k, buf, away(-dx, c), 3 + dx, sibling))
        gather_copy(k, buf, sibling, 3, sibling).wait_recv()
        for dx in (1, 3, 2)[: chips - 1] if chips > 2 else (1,):
            gather_copy(k, buf, away(-dx, 1 - c), 3 + dx, sibling).wait_recv()

    def triangle_copy(xs, q, i, to):
        first = 2 * width * xs // 128 * 128
        part = fac_t.at[rows(q), pl.ds(first, n - first)]
        return copy(part, part, g_send.at[0, i], g_recv.at[0, i], t, to)

    def for_chip(dx, action):
        for xs in range(chips):
            cond = lambda xs=xs: lax.rem(x + chips + dx, chips) == xs
            pl.when(cond())(lambda xs=xs, cond=cond: action(xs, cond))

    def start_triangle():
        def sends(xs, cond):
            for dx in (2, 1, 3):
                send(cond, lambda dx=dx: triangle_copy(xs, p, dx - 1, away(dx, c)))
            send(cond, lambda: triangle_copy(xs, p, 3, sibling))

        for_chip(0, sends)

    def finish_triangle():
        def forward(dx, xs, cond):
            triangle_copy(xs, away(-dx, c), dx - 1, sibling).wait_recv()
            send(cond, lambda: triangle_copy(xs, away(-dx, c), 3 + dx, sibling))

        for dx in (1, 3, 2):
            for_chip(-dx, functools.partial(forward, dx))
        for_chip(0, lambda xs, cond: triangle_copy(xs, sibling, 3, sibling).wait_recv())
        for dx in (1, 3, 2):
            for_chip(-dx, lambda xs, cond, dx=dx: triangle_copy(xs, away(-dx, 1 - c), 3 + dx, sibling).wait_recv())

    def exchange_copy(k, src, dst, j, to):
        return copy(blocks.at[k, src], gathered.at[k, rows(dst)], a_send.at[k, j - 1], a_recv.at[k, j - 1], t, to)

    def start_exchange(k, panel, cond=None):
        wide = jnp.concatenate([panel, panel[:, :128]], axis=1)
        for q in range(panels):
            blocks[k, q] = wide[:, q * width : q * width + 128]
        for j in sorted(range(1, panels), key=lambda j: abs(j - chips)):
            q = lambda j=j: lax.rem(p + j, panels)
            send(cond, lambda j=j, q=q: exchange_copy(k, q(), p, j, q()))
        gathered[k, rows(p)] = blocks[k, p]

    def finish_exchange(k):
        for j in range(1, panels):
            q = lax.rem(p + panels - j, panels)
            exchange_copy(k, q, q, j, q).wait_recv()

    def comp_copy(r, to):
        return copy(comp.at[r, rows(p)], comp_recv.at[r], t_send.at[r, 0], t_recv.at[r, 0], to, p)

    def cov_copy(r, to):
        return copy(cov_send.at[r], cov_recv.at[r], t_send.at[r, 1], t_recv.at[r, 1], to, p)

    def send_comp(r):
        @pl.when(has_target(r))
        def _():
            send(lambda: has_target(r), lambda: comp_copy(r, t - (1 << r)))

    def send_cov(r):
        cov_send[r] = own_cov[...].astype(BF16)

        @pl.when(has_target(r))
        def _():
            send(lambda: has_target(r), lambda: cov_copy(r, t - (1 << r)))

    loads = [
        pltpu.make_async_copy(coupling_ref, coupling_buf, load_sem.at[0]),
        pltpu.make_async_copy(factor_ref, factor_buf, load_sem.at[1]),
    ]
    for load in loads:
        load.start()

    @pl.when(last)
    def _():
        pltpu.make_async_copy(sigma_ref, sigma_buf, load_sem.at[2]).start()

    fac_t[...] = jnp.zeros_like(fac_t)
    barrier = pltpu.get_barrier_semaphore()
    for j in range(1, panels):
        pl.semaphore_signal(barrier, 1, device_id=(t, lax.rem(p + j, panels)), device_id_type=MESH)
    for r in range(rounds):
        @pl.when(has_target(r))
        def _():
            pl.semaphore_signal(barrier, 1, device_id=(t - (1 << r), p), device_id_type=MESH)

        @pl.when(has_source(r))
        def _():
            pl.semaphore_signal(barrier, 1, device_id=(t + (1 << r), p), device_id_type=MESH)

    loads[0].wait()
    comp_t[rows(p)] = coupling_buf[...].astype(BF16)
    loads[1].wait()
    fac_high, fac_low = split(factor_buf[...])
    fac_t[rows(p)] = fac_high

    peers = panels - 1
    for r in range(rounds):
        peers += has_target(r).astype(jnp.int32) + has_source(r).astype(jnp.int32)
    pl.semaphore_wait(barrier, peers)

    start_gather(rounds, lambda: comp_t)
    start_triangle()
    finish_gather(rounds, lambda: comp_t)
    for j in range(n // 128):
        comp[0, :, 128 * j : 128 * (j + 1)] = comp_t[128 * j : 128 * (j + 1), :].T
    send_comp(0)
    finish_triangle()
    own_cov[...] = dot_nt(fac_high, fac_t[...]) + dot_nt(fac_low, fac_t[...])

    @pl.when(last)
    def _():
        pltpu.make_async_copy(sigma_ref, sigma_buf, load_sem.at[2]).wait()
        sig_high, sig_low = split(sigma_buf[...])
        own = comp_t[rows(p)]
        w_high, w_low = split(dot(own, sig_high) + dot(own, sig_low))
        own_cov[...] += dot(w_high, comp[0]) + dot(w_low, comp[0])

    send_cov(0)

    for r in range(rounds):
        active = has_source(r)
        more = r + 1 < rounds
        if r:
            @pl.when(active)
            def _():
                finish_gather(r, lambda r=r: comp.at[r], lambda r=r: has_source(r))

        if more:
            @pl.when(active)
            def _():
                comp_copy(r, t).wait_recv()
                comp[r + 1, rows(p)] = dot(comp_recv[r], comp[r]).astype(BF16)

            @pl.when(jnp.logical_not(active))
            def _():
                comp[r + 1, rows(p)] = comp[r, rows(p)]

            send_comp(r + 1)

            @pl.when(has_source(r + 1))
            def _():
                start_gather(r + 1, lambda r=r: comp.at[r + 1], lambda r=r: has_source(r + 1))
        else:
            @pl.when(active)
            def _():
                comp_copy(r, t).wait_recv()
                start_exchange(rounds, dot(comp_recv[r], comp[r]).astype(BF16), lambda r=r: has_source(r))

            @pl.when(jnp.logical_not(active))
            def _():
                start_exchange(rounds, comp[r, rows(p)], lambda r=r: jnp.logical_not(has_source(r)))

        @pl.when(active)
        def _():
            cov_copy(r, t).wait_recv()
            start_exchange(r, dot(cov_recv[r], comp[r]).astype(BF16), lambda r=r: has_source(r))
            finish_exchange(r)
            middle_t = gathered[r].T[:width]
            own_cov[...] += dot(middle_t, comp[r])

        if more:
            send_cov(r + 1)

    cov_out[...] = own_cov[...]
    finish_exchange(rounds)
    prop_out[...] = gathered[rounds].T[:width]

    for cond, make in pending:
        if cond is None:
            make().wait_send()
        else:
            pl.when(cond())(lambda make=make: make().wait_send())


def shards(factor_inverse, coupling, sigma_after):
    steps, panels = lax.axis_size("tm"), lax.axis_size("panel")
    n, width = factor_inverse.shape[1:]
    rounds = (steps - 1).bit_length()
    chips = panels // 2
    vmem = pl.BlockSpec(memory_space=pltpu.VMEM)
    cov, prop = pl.pallas_call(
        functools.partial(kernel, steps, chips, rounds),
        out_shape=(
            jax.ShapeDtypeStruct((width, n), F32),
            jax.ShapeDtypeStruct((width, n), BF16),
        ),
        in_specs=[pl.BlockSpec(memory_space=pl.ANY)] * 3,
        out_specs=(vmem, vmem),
        scratch_shapes=[
            pltpu.VMEM((rounds, n, n), BF16),
            pltpu.VMEM((n, n), BF16),
            pltpu.VMEM((n, n), BF16),
            pltpu.VMEM((width, n), F32),
            pltpu.VMEM((width, n), F32),
            pltpu.VMEM((width, n), F32),
            pltpu.VMEM((rounds, width, n), BF16),
            pltpu.VMEM((rounds, width, n), BF16),
            pltpu.VMEM((rounds, width, n), BF16),
            pltpu.VMEM((rounds + 1, panels, width, 128), BF16),
            pltpu.VMEM((rounds + 1, n, 128), BF16),
            pltpu.VMEM((n, n), F32),
            pltpu.SemaphoreType.DMA((rounds + 1, 7)),
            pltpu.SemaphoreType.DMA((rounds + 1, 7)),
            pltpu.SemaphoreType.DMA((rounds, 2)),
            pltpu.SemaphoreType.DMA((rounds, 2)),
            pltpu.SemaphoreType.DMA((rounds + 1, panels - 1)),
            pltpu.SemaphoreType.DMA((rounds + 1, panels - 1)),
            pltpu.SemaphoreType.DMA((3,)),
        ],
        compiler_params=pltpu.CompilerParams(
            collective_id=0, has_side_effects=True, vmem_limit_bytes=55_990_000
        ),
        name="scan",
    )(factor_inverse[0].T, coupling[0].T, sigma_after)
    return cov.T[None], prop.T[None]


def solution(mesh):
    placed = (P("tm", None, "panel"), P("tm", None, "panel"), P())
    return jax.shard_map(
        shards,
        mesh=mesh,
        in_specs=placed,
        out_specs=(P("tm", None, "panel"), P("tm", None, "panel")),
        check_vma=False,
    )
```

```python
import functools

import jax
import jax.numpy as jnp
from jax import lax
from jax.experimental import pallas as pl
from jax.experimental.pallas import tpu as pltpu
from jax.sharding import PartitionSpec as P

MESH = pl.DeviceIdType.MESH
F32 = jnp.float32
BF16 = jnp.bfloat16


def dot(a, b):
    return jnp.dot(a, b, preferred_element_type=F32)


def dot_nt(a, b):
    return lax.dot_general(a, b, (((1,), (1,)), ((), ())), preferred_element_type=F32)


def split(a):
    high = a.astype(BF16)
    return high, (a - high.astype(F32)).astype(BF16)


def kernel(
    steps, chips, rounds,
    factor_ref, coupling_ref, sigma_ref, cov_out, prop_out,
    comp, comp_t, fac_t, coupling_buf, factor_buf, own_cov, cov_send, comp_recv, cov_recv, blocks, gathered, sigma_buf,
    g_send, g_recv, t_send, t_recv, a_send, a_recv, load_sem,
):
    width, n = own_cov.shape
    panels = 2 * chips
    t = lax.axis_index("tm")
    p = lax.axis_index("panel")
    x, c = lax.div(p, 2), lax.rem(p, 2)
    sibling = 2 * x + 1 - c
    last = t == steps - 1
    pending = []

    def has_source(r):
        return t + (1 << r) < steps

    def has_target(r):
        return t - (1 << r) >= 0

    def rows(q):
        return pl.ds(pl.multiple_of(q * width, 32), width)

    def away(dx, core):
        return 2 * lax.rem(x + chips + dx, chips) + core

    def send(cond, make):
        make().start()
        pending.append((cond, make))

    def copy(src, dst, s, r, tm, panel):
        return pltpu.make_async_remote_copy(
            src_ref=src, dst_ref=dst, send_sem=s, recv_sem=r, device_id=(tm, panel), device_id_type=MESH
        )

    def drain(sent):
        groups = {}
        for entry in sent:
            pending.remove(entry)
            groups.setdefault(entry[0], []).append(entry[1])
        for cond, makes in groups.items():
            def waits(makes=makes):
                for make in makes:
                    make().wait_send()

            waits() if cond is None else pl.when(cond())(waits)

    source = [lambda r=r: has_source(r) for r in range(rounds)]
    target = [lambda r=r: has_target(r) for r in range(rounds)]

    def gather_copy(k, buf, q, i, to):
        return copy(buf().at[rows(q)], buf().at[rows(q)], g_send.at[k, i], g_recv.at[k, i], t, to)

    def start_gather(k, buf, cond=None):
        for dx in (2, 1, 3)[: chips - 1] if chips > 2 else (1,):
            send(cond, lambda dx=dx: gather_copy(k, buf, p, dx - 1, away(dx, c)))
        send(cond, lambda: gather_copy(k, buf, p, 3, sibling))

    def finish_gather(k, buf, cond=None):
        for dx in (1, 3, 2)[: chips - 1] if chips > 2 else (1,):
            gather_copy(k, buf, away(-dx, c), dx - 1, sibling).wait_recv()
            send(cond, lambda dx=dx: gather_copy(k, buf, away(-dx, c), 3 + dx, sibling))
        gather_copy(k, buf, sibling, 3, sibling).wait_recv()
        for dx in (1, 3, 2)[: chips - 1] if chips > 2 else (1,):
            gather_copy(k, buf, away(-dx, 1 - c), 3 + dx, sibling).wait_recv()

    def triangle_copy(xs, q, i, to):
        first = 2 * width * xs // 128 * 128
        part = fac_t.at[rows(q), pl.ds(first, n - first)]
        return copy(part, part, g_send.at[0, i], g_recv.at[0, i], t, to)

    def for_chip(dx, action):
        for xs in range(chips):
            cond = lambda xs=xs: lax.rem(x + chips + dx, chips) == xs
            pl.when(cond())(lambda xs=xs, cond=cond: action(xs, cond))

    def start_triangle():
        def sends(xs, cond):
            for dx in (2, 1, 3):
                send(cond, lambda dx=dx: triangle_copy(xs, p, dx - 1, away(dx, c)))
            send(cond, lambda: triangle_copy(xs, p, 3, sibling))

        for_chip(0, sends)

    def finish_triangle():
        def forward(dx, xs, cond):
            triangle_copy(xs, away(-dx, c), dx - 1, sibling).wait_recv()
            send(cond, lambda: triangle_copy(xs, away(-dx, c), 3 + dx, sibling))

        for dx in (1, 3, 2):
            for_chip(-dx, functools.partial(forward, dx))
        for_chip(0, lambda xs, cond: triangle_copy(xs, sibling, 3, sibling).wait_recv())
        for dx in (1, 3, 2):
            for_chip(-dx, lambda xs, cond, dx=dx: triangle_copy(xs, away(-dx, 1 - c), 3 + dx, sibling).wait_recv())

    def exchange_copy(k, src, dst, j, to):
        return copy(blocks.at[k, src], gathered.at[k, rows(dst)], a_send.at[k, j - 1], a_recv.at[k, j - 1], t, to)

    def put_blocks(k, panel):
        wide = jnp.concatenate([panel, panel[:, :128]], axis=1)
        for q in range(panels):
            blocks[k, q] = wide[:, q * width : q * width + 128]

    def send_blocks(k, cond=None):
        for j in sorted(range(1, panels), key=lambda j: abs(j - chips)):
            q = lambda j=j: lax.rem(p + j, panels)
            send(cond, lambda j=j, q=q: exchange_copy(k, q(), p, j, q()))
        gathered[k, rows(p)] = blocks[k, p]

    def start_exchange(k, panel, cond=None):
        put_blocks(k, panel)
        send_blocks(k, cond)

    def finish_exchange(k):
        for j in range(1, panels):
            q = lax.rem(p + panels - j, panels)
            exchange_copy(k, q, q, j, q).wait_recv()

    def comp_copy(r, to):
        return copy(comp.at[r, rows(p)], comp_recv.at[r], t_send.at[r, 0], t_recv.at[r, 0], to, p)

    def cov_copy(r, to):
        return copy(cov_send.at[r], cov_recv.at[r], t_send.at[r, 1], t_recv.at[r, 1], to, p)

    def send_comp(r):
        @pl.when(has_target(r))
        def _():
            send(target[r], lambda: comp_copy(r, t - (1 << r)))

    def send_cov(r):
        cov_send[r] = own_cov[...].astype(BF16)

        @pl.when(has_target(r))
        def _():
            send(target[r], lambda: cov_copy(r, t - (1 << r)))

    loads = [
        pltpu.make_async_copy(coupling_ref, coupling_buf, load_sem.at[0]),
        pltpu.make_async_copy(factor_ref, factor_buf, load_sem.at[1]),
    ]
    for load in loads:
        load.start()

    @pl.when(last)
    def _():
        pltpu.make_async_copy(sigma_ref, sigma_buf, load_sem.at[2]).start()

    fac_t[...] = jnp.zeros_like(fac_t)
    barrier = pltpu.get_barrier_semaphore()
    for j in range(1, panels):
        pl.semaphore_signal(barrier, 1, device_id=(t, lax.rem(p + j, panels)), device_id_type=MESH)
    for r in range(rounds):
        @pl.when(has_target(r))
        def _():
            pl.semaphore_signal(barrier, 1, device_id=(t - (1 << r), p), device_id_type=MESH)

        @pl.when(has_source(r))
        def _():
            pl.semaphore_signal(barrier, 1, device_id=(t + (1 << r), p), device_id_type=MESH)

    loads[0].wait()
    comp_t[rows(p)] = coupling_buf[...].astype(BF16)
    loads[1].wait()
    fac_high, fac_low = split(factor_buf[...])
    fac_t[rows(p)] = fac_high

    peers = panels - 1
    for r in range(rounds):
        peers += has_target(r).astype(jnp.int32) + has_source(r).astype(jnp.int32)
    pl.semaphore_wait(barrier, peers)

    start_gather(rounds, lambda: comp_t)
    start_triangle()
    finish_gather(rounds, lambda: comp_t)
    for j in range(n // 128):
        comp[0, :, 128 * j : 128 * (j + 1)] = comp_t[128 * j : 128 * (j + 1), :].T
    send_comp(0)
    finish_triangle()
    own_cov[...] = dot_nt(fac_high, fac_t[...]) + dot_nt(fac_low, fac_t[...])

    @pl.when(last)
    def _():
        pltpu.make_async_copy(sigma_ref, sigma_buf, load_sem.at[2]).wait()
        sig_high, sig_low = split(sigma_buf[...])
        own = comp_t[rows(p)]
        w_high, w_low = split(dot(own, sig_high) + dot(own, sig_low))
        own_cov[...] += dot(w_high, comp[0]) + dot(w_low, comp[0])

    send_cov(0)

    for r in range(rounds):
        active = has_source(r)
        more = r + 1 < rounds
        old = pending[:-1]
        if r:
            @pl.when(active)
            def _():
                finish_gather(r, lambda r=r: comp.at[r], source[r])

        @pl.when(active)
        def _():
            comp_copy(r, t).wait_recv()
            panel = dot(comp_recv[r], comp[r]).astype(BF16)
            if more:
                comp[r + 1, rows(p)] = panel
            else:
                put_blocks(rounds, panel)

        @pl.when(jnp.logical_not(active))
        def _():
            if more:
                comp[r + 1, rows(p)] = comp[r, rows(p)]
            else:
                put_blocks(rounds, comp[r, rows(p)])

        if more:
            send_comp(r + 1)

            @pl.when(has_source(r + 1))
            def _():
                start_gather(r + 1, lambda r=r: comp.at[r + 1], source[r + 1])
        else:
            send_blocks(rounds)

        drain(old)

        @pl.when(active)
        def _():
            cov_copy(r, t).wait_recv()
            start_exchange(r, dot(cov_recv[r], comp[r]).astype(BF16), source[r])

        if not more:
            finish_exchange(rounds)
            prop_out[...] = gathered[rounds].T[:width]

        @pl.when(active)
        def _():
            finish_exchange(r)
            own_cov[...] += dot(gathered[r].T[:width], comp[r])

        if more:
            send_cov(r + 1)

    cov_out[...] = own_cov[...]
    drain(pending[:])


def shards(factor_inverse, coupling, sigma_after):
    steps, panels = lax.axis_size("tm"), lax.axis_size("panel")
    n, width = factor_inverse.shape[1:]
    rounds = (steps - 1).bit_length()
    chips = panels // 2
    vmem = pl.BlockSpec(memory_space=pltpu.VMEM)
    cov, prop = pl.pallas_call(
        functools.partial(kernel, steps, chips, rounds),
        out_shape=(
            jax.ShapeDtypeStruct((width, n), F32),
            jax.ShapeDtypeStruct((width, n), BF16),
        ),
        in_specs=[pl.BlockSpec(memory_space=pl.ANY)] * 3,
        out_specs=(vmem, vmem),
        scratch_shapes=[
            pltpu.VMEM((rounds, n, n), BF16),
            pltpu.VMEM((n, n), BF16),
            pltpu.VMEM((n, n), BF16),
            pltpu.VMEM((width, n), F32),
            pltpu.VMEM((width, n), F32),
            pltpu.VMEM((width, n), F32),
            pltpu.VMEM((rounds, width, n), BF16),
            pltpu.VMEM((rounds, width, n), BF16),
            pltpu.VMEM((rounds, width, n), BF16),
            pltpu.VMEM((rounds + 1, panels, width, 128), BF16),
            pltpu.VMEM((rounds + 1, n, 128), BF16),
            pltpu.VMEM((n, n), F32),
            pltpu.SemaphoreType.DMA((rounds + 1, 7)),
            pltpu.SemaphoreType.DMA((rounds + 1, 7)),
            pltpu.SemaphoreType.DMA((rounds, 2)),
            pltpu.SemaphoreType.DMA((rounds, 2)),
            pltpu.SemaphoreType.DMA((rounds + 1, panels - 1)),
            pltpu.SemaphoreType.DMA((rounds + 1, panels - 1)),
            pltpu.SemaphoreType.DMA((3,)),
        ],
        compiler_params=pltpu.CompilerParams(
            collective_id=0, has_side_effects=True, vmem_limit_bytes=55_990_000
        ),
        name="scan",
    )(factor_inverse[0].T, coupling[0].T, sigma_after)
    return cov.T[None], prop.T[None]


def solution(mesh):
    placed = (P("tm", None, "panel"), P("tm", None, "panel"), P())
    return jax.shard_map(
        shards,
        mesh=mesh,
        in_specs=placed,
        out_specs=(P("tm", None, "panel"), P("tm", None, "panel")),
        check_vma=False,
    )
```

```python
import functools

import jax
import jax.numpy as jnp
from jax import lax
from jax.experimental import pallas as pl
from jax.experimental.pallas import tpu as pltpu
from jax.sharding import PartitionSpec as P

MESH = pl.DeviceIdType.MESH
F32 = jnp.float32
BF16 = jnp.bfloat16


def dot(a, b):
    return jnp.dot(a, b, preferred_element_type=F32)


def dot_nt(a, b):
    return lax.dot_general(a, b, (((1,), (1,)), ((), ())), preferred_element_type=F32)


def split(a):
    high = a.astype(BF16)
    return high, (a - high.astype(F32)).astype(BF16)


def kernel(
    steps, chips, rounds,
    factor_ref, coupling_ref, sigma_ref, cov_out, prop_out,
    comp, comp_t, fac_t, coupling_buf, factor_buf, own_cov, cov_send, comp_recv, cov_recv, blocks, gathered, sigma_buf,
    g_send, g_recv, t_send, t_recv, a_send, a_recv, load_sem,
):
    width, n = own_cov.shape
    panels = 2 * chips
    t = lax.axis_index("tm")
    p = lax.axis_index("panel")
    x, c = lax.div(p, 2), lax.rem(p, 2)
    sibling = 2 * x + 1 - c
    last = t == steps - 1
    pending = []

    def has_source(r):
        return t + (1 << r) < steps

    def has_target(r):
        return t - (1 << r) >= 0

    def rows(q):
        return pl.ds(pl.multiple_of(q * width, 32), width)

    def away(dx, core):
        return 2 * lax.rem(x + chips + dx, chips) + core

    def send(cond, make):
        make().start()
        pending.append((cond, make))

    def copy(src, dst, s, r, tm, panel):
        return pltpu.make_async_remote_copy(
            src_ref=src, dst_ref=dst, send_sem=s, recv_sem=r, device_id=(tm, panel), device_id_type=MESH
        )

    def drain(sent):
        groups = {}
        for entry in sent:
            pending.remove(entry)
            groups.setdefault(entry[0], []).append(entry[1])
        for cond, makes in groups.items():
            def waits(makes=makes):
                for make in makes:
                    make().wait_send()

            waits() if cond is None else pl.when(cond())(waits)

    source = [lambda r=r: has_source(r) for r in range(rounds)]
    target = [lambda r=r: has_target(r) for r in range(rounds)]

    def gather_copy(k, buf, q, i, to):
        return copy(buf().at[rows(q)], buf().at[rows(q)], g_send.at[k, i], g_recv.at[k, i], t, to)

    def start_gather(k, buf, cond=None):
        for dx in (2, 1, 3)[: chips - 1] if chips > 2 else (1,):
            send(cond, lambda dx=dx: gather_copy(k, buf, p, dx - 1, away(dx, c)))
        send(cond, lambda: gather_copy(k, buf, p, 3, sibling))

    def near_gather(k, buf, cond=None):
        for dx in (1, 3):
            gather_copy(k, buf, away(-dx, c), dx - 1, sibling).wait_recv()
            send(cond, lambda dx=dx: gather_copy(k, buf, away(-dx, c), 3 + dx, sibling))

    def finish_gather(k, buf, cond=None, order=(2,)):
        for dx in order:
            gather_copy(k, buf, away(-dx, c), dx - 1, sibling).wait_recv()
            send(cond, lambda dx=dx: gather_copy(k, buf, away(-dx, c), 3 + dx, sibling))
        gather_copy(k, buf, sibling, 3, sibling).wait_recv()
        for dx in (1, 3, 2)[: chips - 1] if chips > 2 else (1,):
            gather_copy(k, buf, away(-dx, 1 - c), 3 + dx, sibling).wait_recv()

    def triangle_copy(xs, q, i, to):
        first = 2 * width * xs // 128 * 128
        part = fac_t.at[rows(q), pl.ds(first, n - first)]
        return copy(part, part, g_send.at[0, i], g_recv.at[0, i], t, to)

    def for_chip(dx, action):
        for xs in range(chips):
            cond = lambda xs=xs: lax.rem(x + chips + dx, chips) == xs
            pl.when(cond())(lambda xs=xs, cond=cond: action(xs, cond))

    def start_triangle():
        def sends(xs, cond):
            for dx in (2, 1, 3):
                send(cond, lambda dx=dx: triangle_copy(xs, p, dx - 1, away(dx, c)))
            send(cond, lambda: triangle_copy(xs, p, 3, sibling))

        for_chip(0, sends)

    def finish_triangle():
        def forward(dx, xs, cond):
            triangle_copy(xs, away(-dx, c), dx - 1, sibling).wait_recv()
            send(cond, lambda: triangle_copy(xs, away(-dx, c), 3 + dx, sibling))

        for dx in (1, 3, 2):
            for_chip(-dx, functools.partial(forward, dx))
        for_chip(0, lambda xs, cond: triangle_copy(xs, sibling, 3, sibling).wait_recv())
        for dx in (1, 3, 2):
            for_chip(-dx, lambda xs, cond, dx=dx: triangle_copy(xs, away(-dx, 1 - c), 3 + dx, sibling).wait_recv())

    def exchange_copy(k, src, dst, j, to):
        return copy(blocks.at[k, src], gathered.at[k, rows(dst)], a_send.at[k, j - 1], a_recv.at[k, j - 1], t, to)

    def put_blocks(k, panel):
        wide = jnp.concatenate([panel, panel[:, :128]], axis=1)
        for q in range(panels):
            blocks[k, q] = wide[:, q * width : q * width + 128]

    def send_blocks(k, cond=None):
        for j in sorted(range(1, panels), key=lambda j: abs(j - chips)):
            q = lambda j=j: lax.rem(p + j, panels)
            send(cond, lambda j=j, q=q: exchange_copy(k, q(), p, j, q()))
        gathered[k, rows(p)] = blocks[k, p]

    def start_exchange(k, panel, cond=None):
        put_blocks(k, panel)
        send_blocks(k, cond)

    def finish_exchange(k):
        for j in range(1, panels):
            q = lax.rem(p + panels - j, panels)
            exchange_copy(k, q, q, j, q).wait_recv()

    def comp_copy(r, to):
        return copy(comp.at[r, rows(p)], comp_recv.at[r], t_send.at[r, 0], t_recv.at[r, 0], to, p)

    def cov_copy(r, to):
        return copy(cov_send.at[r], cov_recv.at[r], t_send.at[r, 1], t_recv.at[r, 1], to, p)

    def send_comp(r):
        @pl.when(has_target(r))
        def _():
            send(target[r], lambda: comp_copy(r, t - (1 << r)))

    def send_cov(r):
        cov_send[r] = own_cov[...].astype(BF16)

        @pl.when(has_target(r))
        def _():
            send(target[r], lambda: cov_copy(r, t - (1 << r)))

    loads = [
        pltpu.make_async_copy(coupling_ref, coupling_buf, load_sem.at[0]),
        pltpu.make_async_copy(factor_ref, factor_buf, load_sem.at[1]),
    ]
    for load in loads:
        load.start()

    @pl.when(last)
    def _():
        pltpu.make_async_copy(sigma_ref, sigma_buf, load_sem.at[2]).start()

    fac_t[...] = jnp.zeros_like(fac_t)
    barrier = pltpu.get_barrier_semaphore()
    for j in range(1, panels):
        pl.semaphore_signal(barrier, 1, device_id=(t, lax.rem(p + j, panels)), device_id_type=MESH)
    for r in range(rounds):
        @pl.when(has_target(r))
        def _():
            pl.semaphore_signal(barrier, 1, device_id=(t - (1 << r), p), device_id_type=MESH)

        @pl.when(has_source(r))
        def _():
            pl.semaphore_signal(barrier, 1, device_id=(t + (1 << r), p), device_id_type=MESH)

    loads[0].wait()
    comp_t[rows(p)] = coupling_buf[...].astype(BF16)
    loads[1].wait()
    fac_high, fac_low = split(factor_buf[...])
    fac_t[rows(p)] = fac_high

    peers = panels - 1
    for r in range(rounds):
        peers += has_target(r).astype(jnp.int32) + has_source(r).astype(jnp.int32)
    pl.semaphore_wait(barrier, peers)

    start_gather(rounds, lambda: comp_t)
    start_triangle()
    finish_gather(rounds, lambda: comp_t, None, (1, 3, 2))
    for j in range(n // 128):
        comp[0, :, 128 * j : 128 * (j + 1)] = comp_t[128 * j : 128 * (j + 1), :].T
    send_comp(0)
    finish_triangle()
    both = dot_nt(jnp.concatenate([fac_high, fac_low]), fac_t[...])
    own_cov[...] = both[:width] + both[width:]

    @pl.when(last)
    def _():
        pltpu.make_async_copy(sigma_ref, sigma_buf, load_sem.at[2]).wait()
        sig_high, sig_low = split(sigma_buf[...])
        own = comp_t[rows(p)]
        w_high, w_low = split(dot(own, sig_high) + dot(own, sig_low))
        own_cov[...] += dot(w_high, comp[0]) + dot(w_low, comp[0])

    send_cov(0)

    for r in range(rounds):
        active = has_source(r)
        more = r + 1 < rounds
        old = pending[:-1]
        if r:
            @pl.when(active)
            def _():
                finish_gather(r, lambda r=r: comp.at[r], source[r])

        @pl.when(active)
        def _():
            comp_copy(r, t).wait_recv()
            panel = dot(comp_recv[r], comp[r]).astype(BF16)
            if more:
                comp[r + 1, rows(p)] = panel
            else:
                put_blocks(rounds, panel)

        @pl.when(jnp.logical_not(active))
        def _():
            if more:
                comp[r + 1, rows(p)] = comp[r, rows(p)]
            else:
                put_blocks(rounds, comp[r, rows(p)])

        if more:
            send_comp(r + 1)

            @pl.when(has_source(r + 1))
            def _():
                start_gather(r + 1, lambda r=r: comp.at[r + 1], source[r + 1])
        else:
            send_blocks(rounds)

        drain(old)

        @pl.when(active)
        def _():
            cov_copy(r, t).wait_recv()
            start_exchange(r, dot(cov_recv[r], comp[r]).astype(BF16), source[r])

        if more:
            @pl.when(has_source(r + 1))
            def _():
                near_gather(r + 1, lambda r=r: comp.at[r + 1], source[r + 1])

        if not more:
            finish_exchange(rounds)
            prop_out[...] = gathered[rounds].T[:width]

        @pl.when(active)
        def _():
            finish_exchange(r)
            own_cov[...] += dot(gathered[r].T[:width], comp[r])

        if more:
            send_cov(r + 1)

    cov_out[...] = own_cov[...]
    drain(pending[:])


def shards(factor_inverse, coupling, sigma_after):
    steps, panels = lax.axis_size("tm"), lax.axis_size("panel")
    n, width = factor_inverse.shape[1:]
    rounds = (steps - 1).bit_length()
    chips = panels // 2
    vmem = pl.BlockSpec(memory_space=pltpu.VMEM)
    cov, prop = pl.pallas_call(
        functools.partial(kernel, steps, chips, rounds),
        out_shape=(
            jax.ShapeDtypeStruct((width, n), F32),
            jax.ShapeDtypeStruct((width, n), BF16),
        ),
        in_specs=[pl.BlockSpec(memory_space=pl.ANY)] * 3,
        out_specs=(vmem, vmem),
        scratch_shapes=[
            pltpu.VMEM((rounds, n, n), BF16),
            pltpu.VMEM((n, n), BF16),
            pltpu.VMEM((n, n), BF16),
            pltpu.VMEM((width, n), F32),
            pltpu.VMEM((width, n), F32),
            pltpu.VMEM((width, n), F32),
            pltpu.VMEM((rounds, width, n), BF16),
            pltpu.VMEM((rounds, width, n), BF16),
            pltpu.VMEM((rounds, width, n), BF16),
            pltpu.VMEM((rounds + 1, panels, width, 128), BF16),
            pltpu.VMEM((rounds + 1, n, 128), BF16),
            pltpu.VMEM((n, n), F32),
            pltpu.SemaphoreType.DMA((rounds + 1, 7)),
            pltpu.SemaphoreType.DMA((rounds + 1, 7)),
            pltpu.SemaphoreType.DMA((rounds, 2)),
            pltpu.SemaphoreType.DMA((rounds, 2)),
            pltpu.SemaphoreType.DMA((rounds + 1, panels - 1)),
            pltpu.SemaphoreType.DMA((rounds + 1, panels - 1)),
            pltpu.SemaphoreType.DMA((3,)),
        ],
        compiler_params=pltpu.CompilerParams(
            collective_id=0, has_side_effects=True, vmem_limit_bytes=55_990_000
        ),
        name="scan",
    )(factor_inverse[0].T, coupling[0].T, sigma_after)
    return cov.T[None], prop.T[None]


def solution(mesh):
    placed = (P("tm", None, "panel"), P("tm", None, "panel"), P())
    return jax.shard_map(
        shards,
        mesh=mesh,
        in_specs=placed,
        out_specs=(P("tm", None, "panel"), P("tm", None, "panel")),
        check_vma=False,
    )
```

```python
import functools

import jax
import jax.numpy as jnp
from jax import lax
from jax.experimental import pallas as pl
from jax.experimental.pallas import tpu as pltpu
from jax.sharding import PartitionSpec as P

MESH = pl.DeviceIdType.MESH
F32 = jnp.float32
BF16 = jnp.bfloat16


def dot(a, b):
    return jnp.dot(a, b, preferred_element_type=F32)


def dot_nt(a, b):
    return lax.dot_general(a, b, (((1,), (1,)), ((), ())), preferred_element_type=F32)


def split(a):
    high = a.astype(BF16)
    return high, (a - high.astype(F32)).astype(BF16)


def kernel(
    steps, chips, rounds,
    factor_ref, coupling_ref, sigma_ref, cov_out, prop_out,
    comp, comp_t, fac_t, coupling_buf, factor_buf, own_cov, cov_send, comp_recv, cov_recv, blocks, gathered, sigma_buf,
    g_send, g_recv, t_send, t_recv, a_send, a_recv, load_sem,
):
    width, n = own_cov.shape
    panels = 2 * chips
    t = lax.axis_index("tm")
    p = lax.axis_index("panel")
    x, c = lax.div(p, 2), lax.rem(p, 2)
    sibling = 2 * x + 1 - c
    last = t == steps - 1
    pending = []

    def has_source(r):
        return t + (1 << r) < steps

    def has_target(r):
        return t - (1 << r) >= 0

    def rows(q):
        return pl.ds(pl.multiple_of(q * width, 32), width)

    def away(dx, core):
        return 2 * lax.rem(x + chips + dx, chips) + core

    def send(cond, make):
        make().start()
        pending.append((cond, make))

    def copy(src, dst, s, r, tm, panel):
        return pltpu.make_async_remote_copy(
            src_ref=src, dst_ref=dst, send_sem=s, recv_sem=r, device_id=(tm, panel), device_id_type=MESH
        )

    def drain(sent):
        groups = {}
        for entry in sent:
            pending.remove(entry)
            groups.setdefault(entry[0], []).append(entry[1])
        for cond, makes in groups.items():
            def waits(makes=makes):
                for make in makes:
                    make().wait_send()

            waits() if cond is None else pl.when(cond())(waits)

    source = [lambda r=r: has_source(r) for r in range(rounds)]
    target = [lambda r=r: has_target(r) for r in range(rounds)]

    def gather_copy(k, buf, q, i, to):
        return copy(buf().at[rows(q)], buf().at[rows(q)], g_send.at[k, i], g_recv.at[k, i], t, to)

    def start_gather(k, buf, cond=None, direct=False):
        for dx in (2, 1, 3) if direct else (1, 3):
            send(cond, lambda dx=dx: gather_copy(k, buf, p, dx - 1, away(dx, c)))
        send(cond, lambda: gather_copy(k, buf, p, 3, sibling))

    def near_gather(k, buf, cond=None):
        for side in (1, -1):
            q = lambda side=side: away(side * (2 * c - 1), c)
            i = lambda side=side: 1 + side * (2 * c - 1)
            gather_copy(k, buf, q(), i(), sibling).wait_recv()
            if side == 1:
                send(cond, lambda q=q: gather_copy(k, buf, q(), 1, away(1 - 2 * c, c)))
            send(cond, lambda q=q, i=i: gather_copy(k, buf, q(), 4 + i(), sibling))

    def finish_gather(k, buf, cond=None, order=(2,)):
        for dx in order:
            gather_copy(k, buf, away(-dx, c), dx - 1, sibling).wait_recv()
            send(cond, lambda dx=dx: gather_copy(k, buf, away(-dx, c), 3 + dx, sibling))
        gather_copy(k, buf, sibling, 3, sibling).wait_recv()
        for dx in (1, 3, 2)[: chips - 1] if chips > 2 else (1,):
            gather_copy(k, buf, away(-dx, 1 - c), 3 + dx, sibling).wait_recv()

    def triangle_copy(xs, q, i, to):
        first = 2 * width * xs // 128 * 128
        part = fac_t.at[rows(q), pl.ds(first, n - first)]
        return copy(part, part, g_send.at[0, i], g_recv.at[0, i], t, to)

    def for_chip(dx, action):
        for xs in range(chips):
            cond = lambda xs=xs: lax.rem(x + chips + dx, chips) == xs
            pl.when(cond())(lambda xs=xs, cond=cond: action(xs, cond))

    def start_triangle():
        def sends(xs, cond):
            for dx in (2, 1, 3):
                send(cond, lambda dx=dx: triangle_copy(xs, p, dx - 1, away(dx, c)))
            send(cond, lambda: triangle_copy(xs, p, 3, sibling))

        for_chip(0, sends)

    def finish_triangle():
        def forward(dx, xs, cond):
            triangle_copy(xs, away(-dx, c), dx - 1, sibling).wait_recv()
            send(cond, lambda: triangle_copy(xs, away(-dx, c), 3 + dx, sibling))

        for dx in (1, 3, 2):
            for_chip(-dx, functools.partial(forward, dx))
        for_chip(0, lambda xs, cond: triangle_copy(xs, sibling, 3, sibling).wait_recv())
        for dx in (1, 3, 2):
            for_chip(-dx, lambda xs, cond, dx=dx: triangle_copy(xs, away(-dx, 1 - c), 3 + dx, sibling).wait_recv())

    def exchange_copy(k, src, dst, j, to):
        return copy(blocks.at[k, src], gathered.at[k, rows(dst)], a_send.at[k, j - 1], a_recv.at[k, j - 1], t, to)

    def put_blocks(k, panel):
        wide = jnp.concatenate([panel, panel[:, :128]], axis=1)
        for q in range(panels):
            blocks[k, q] = wide[:, q * width : q * width + 128]

    def send_blocks(k, cond=None):
        for j in sorted(range(1, panels), key=lambda j: abs(j - chips)):
            q = lambda j=j: lax.rem(p + j, panels)
            send(cond, lambda j=j, q=q: exchange_copy(k, q(), p, j, q()))
        gathered[k, rows(p)] = blocks[k, p]

    def start_exchange(k, panel, cond=None):
        put_blocks(k, panel)
        send_blocks(k, cond)

    def finish_exchange(k):
        for j in range(1, panels):
            q = lax.rem(p + panels - j, panels)
            exchange_copy(k, q, q, j, q).wait_recv()

    def comp_copy(r, to):
        return copy(comp.at[r, rows(p)], comp_recv.at[r], t_send.at[r, 0], t_recv.at[r, 0], to, p)

    def cov_copy(r, to):
        return copy(cov_send.at[r], cov_recv.at[r], t_send.at[r, 1], t_recv.at[r, 1], to, p)

    def send_comp(r):
        @pl.when(has_target(r))
        def _():
            send(target[r], lambda: comp_copy(r, t - (1 << r)))

    def send_cov(r):
        cov_send[r] = own_cov[...].astype(BF16)

        @pl.when(has_target(r))
        def _():
            send(target[r], lambda: cov_copy(r, t - (1 << r)))

    loads = [
        pltpu.make_async_copy(coupling_ref, coupling_buf, load_sem.at[0]),
        pltpu.make_async_copy(factor_ref, factor_buf, load_sem.at[1]),
    ]
    for load in loads:
        load.start()

    @pl.when(last)
    def _():
        pltpu.make_async_copy(sigma_ref, sigma_buf, load_sem.at[2]).start()

    fac_t[...] = jnp.zeros_like(fac_t)
    barrier = pltpu.get_barrier_semaphore()
    for j in range(1, panels):
        pl.semaphore_signal(barrier, 1, device_id=(t, lax.rem(p + j, panels)), device_id_type=MESH)
    for r in range(rounds):
        @pl.when(has_target(r))
        def _():
            pl.semaphore_signal(barrier, 1, device_id=(t - (1 << r), p), device_id_type=MESH)

        @pl.when(has_source(r))
        def _():
            pl.semaphore_signal(barrier, 1, device_id=(t + (1 << r), p), device_id_type=MESH)

    loads[0].wait()
    comp_t[rows(p)] = coupling_buf[...].astype(BF16)
    loads[1].wait()
    fac_high, fac_low = split(factor_buf[...])
    fac_t[rows(p)] = fac_high

    peers = panels - 1
    for r in range(rounds):
        peers += has_target(r).astype(jnp.int32) + has_source(r).astype(jnp.int32)
    pl.semaphore_wait(barrier, peers)

    start_gather(rounds, lambda: comp_t, None, True)
    start_triangle()
    finish_gather(rounds, lambda: comp_t, None, (1, 3, 2))
    for j in range(n // 128):
        comp[0, :, 128 * j : 128 * (j + 1)] = comp_t[128 * j : 128 * (j + 1), :].T
    send_comp(0)
    finish_triangle()
    both = dot_nt(jnp.concatenate([fac_high, fac_low]), fac_t[...])
    own_cov[...] = both[:width] + both[width:]

    @pl.when(last)
    def _():
        pltpu.make_async_copy(sigma_ref, sigma_buf, load_sem.at[2]).wait()
        sig_high, sig_low = split(sigma_buf[...])
        own = comp_t[rows(p)]
        w_high, w_low = split(dot(own, sig_high) + dot(own, sig_low))
        own_cov[...] += dot(w_high, comp[0]) + dot(w_low, comp[0])

    send_cov(0)

    for r in range(rounds):
        active = has_source(r)
        more = r + 1 < rounds
        old = pending[:-1]
        if r:
            @pl.when(active)
            def _():
                finish_gather(r, lambda r=r: comp.at[r], source[r])

        @pl.when(active)
        def _():
            comp_copy(r, t).wait_recv()
            panel = dot(comp_recv[r], comp[r]).astype(BF16)
            if more:
                comp[r + 1, rows(p)] = panel
            else:
                put_blocks(rounds, panel)

        @pl.when(jnp.logical_not(active))
        def _():
            if more:
                comp[r + 1, rows(p)] = comp[r, rows(p)]
            else:
                put_blocks(rounds, comp[r, rows(p)])

        if more:
            send_comp(r + 1)

            @pl.when(has_source(r + 1))
            def _():
                start_gather(r + 1, lambda r=r: comp.at[r + 1], source[r + 1])
        else:
            send_blocks(rounds)

        drain(old)

        @pl.when(active)
        def _():
            cov_copy(r, t).wait_recv()
            start_exchange(r, dot(cov_recv[r], comp[r]).astype(BF16), source[r])

        if more:
            @pl.when(has_source(r + 1))
            def _():
                near_gather(r + 1, lambda r=r: comp.at[r + 1], source[r + 1])

        if not more:
            finish_exchange(rounds)
            prop_out[...] = gathered[rounds].T[:width]

        @pl.when(active)
        def _():
            finish_exchange(r)
            own_cov[...] += dot(gathered[r].T[:width], comp[r])

        if more:
            send_cov(r + 1)

    cov_out[...] = own_cov[...]
    drain(pending[:])


def shards(factor_inverse, coupling, sigma_after):
    steps, panels = lax.axis_size("tm"), lax.axis_size("panel")
    n, width = factor_inverse.shape[1:]
    rounds = (steps - 1).bit_length()
    chips = panels // 2
    vmem = pl.BlockSpec(memory_space=pltpu.VMEM)
    cov, prop = pl.pallas_call(
        functools.partial(kernel, steps, chips, rounds),
        out_shape=(
            jax.ShapeDtypeStruct((width, n), F32),
            jax.ShapeDtypeStruct((width, n), BF16),
        ),
        in_specs=[pl.BlockSpec(memory_space=pl.ANY)] * 3,
        out_specs=(vmem, vmem),
        scratch_shapes=[
            pltpu.VMEM((rounds, n, n), BF16),
            pltpu.VMEM((n, n), BF16),
            pltpu.VMEM((n, n), BF16),
            pltpu.VMEM((width, n), F32),
            pltpu.VMEM((width, n), F32),
            pltpu.VMEM((width, n), F32),
            pltpu.VMEM((rounds, width, n), BF16),
            pltpu.VMEM((rounds, width, n), BF16),
            pltpu.VMEM((rounds, width, n), BF16),
            pltpu.VMEM((rounds + 1, panels, width, 128), BF16),
            pltpu.VMEM((rounds + 1, n, 128), BF16),
            pltpu.VMEM((n, n), F32),
            pltpu.SemaphoreType.DMA((rounds + 1, 7)),
            pltpu.SemaphoreType.DMA((rounds + 1, 7)),
            pltpu.SemaphoreType.DMA((rounds, 2)),
            pltpu.SemaphoreType.DMA((rounds, 2)),
            pltpu.SemaphoreType.DMA((rounds + 1, panels - 1)),
            pltpu.SemaphoreType.DMA((rounds + 1, panels - 1)),
            pltpu.SemaphoreType.DMA((3,)),
        ],
        compiler_params=pltpu.CompilerParams(
            collective_id=0, has_side_effects=True, vmem_limit_bytes=55_990_000
        ),
        name="scan",
    )(factor_inverse[0].T, coupling[0].T, sigma_after)
    return cov.T[None], prop.T[None]


def solution(mesh):
    placed = (P("tm", None, "panel"), P("tm", None, "panel"), P())
    return jax.shard_map(
        shards,
        mesh=mesh,
        in_specs=placed,
        out_specs=(P("tm", None, "panel"), P("tm", None, "panel")),
        check_vma=False,
    )
```

```python
import functools

import jax
import jax.numpy as jnp
from jax import lax
from jax.experimental import pallas as pl
from jax.experimental.pallas import tpu as pltpu
from jax.sharding import PartitionSpec as P

MESH = pl.DeviceIdType.MESH
F32 = jnp.float32
BF16 = jnp.bfloat16


def dot(a, b):
    return jnp.dot(a, b, preferred_element_type=F32)


def dot_nt(a, b):
    return lax.dot_general(a, b, (((1,), (1,)), ((), ())), preferred_element_type=F32)


def split(a):
    high = a.astype(BF16)
    return high, (a - high.astype(F32)).astype(BF16)


def kernel(
    steps, chips, rounds,
    factor_ref, coupling_ref, sigma_ref, cov_out, prop_out,
    comp, comp_t, fac_t, coupling_buf, factor_buf, own_cov, cov_send, comp_recv, cov_recv, blocks, gathered, sigma_buf,
    g_send, g_recv, t_send, t_recv, a_send, a_recv, load_sem,
):
    width, n = own_cov.shape
    panels = 2 * chips
    t = lax.axis_index("tm")
    p = lax.axis_index("panel")
    x, c = lax.div(p, 2), lax.rem(p, 2)
    sibling = 2 * x + 1 - c
    last = t == steps - 1
    pending = []

    def has_source(r):
        return t + (1 << r) < steps

    def has_target(r):
        return t - (1 << r) >= 0

    def rows(q):
        return pl.ds(pl.multiple_of(q * width, 32), width)

    def away(dx, core):
        return 2 * lax.rem(x + chips + dx, chips) + core

    def send(cond, make):
        make().start()
        pending.append((cond, make))

    def copy(src, dst, s, r, tm, panel):
        return pltpu.make_async_remote_copy(
            src_ref=src, dst_ref=dst, send_sem=s, recv_sem=r, device_id=(tm, panel), device_id_type=MESH
        )

    def drain(sent):
        groups = {}
        for entry in sent:
            pending.remove(entry)
            groups.setdefault(entry[0], []).append(entry[1])
        for cond, makes in groups.items():
            def waits(makes=makes):
                for make in makes:
                    make().wait_send()

            waits() if cond is None else pl.when(cond())(waits)

    source = [lambda r=r: has_source(r) for r in range(rounds)]
    target = [lambda r=r: has_target(r) for r in range(rounds)]

    def gather_copy(k, buf, q, i, to):
        return copy(buf().at[rows(q)], buf().at[rows(q)], g_send.at[k, i], g_recv.at[k, i], t, to)

    def start_gather(k, buf, cond=None, direct=False):
        for dx in (2, 1, 3) if direct else (1, 3):
            send(cond, lambda dx=dx: gather_copy(k, buf, p, dx - 1, away(dx, c)))
        send(cond, lambda: gather_copy(k, buf, p, 3, sibling))

    def near_gather(k, buf, cond=None):
        for side in (1, -1):
            q = lambda side=side: away(side * (2 * c - 1), c)
            i = lambda side=side: 1 + side * (2 * c - 1)
            gather_copy(k, buf, q(), i(), sibling).wait_recv()
            if side == 1:
                send(cond, lambda q=q: gather_copy(k, buf, q(), 1, away(1 - 2 * c, c)))
            send(cond, lambda q=q, i=i: gather_copy(k, buf, q(), 4 + i(), sibling))

    def finish_gather(k, buf, cond=None, order=(2,)):
        for dx in order:
            gather_copy(k, buf, away(-dx, c), dx - 1, sibling).wait_recv()
            send(cond, lambda dx=dx: gather_copy(k, buf, away(-dx, c), 3 + dx, sibling))
        gather_copy(k, buf, sibling, 3, sibling).wait_recv()
        for dx in (1, 3, 2)[: chips - 1] if chips > 2 else (1,):
            gather_copy(k, buf, away(-dx, 1 - c), 3 + dx, sibling).wait_recv()

    def triangle_copy(xs, q, i, to):
        first = 2 * width * xs // 128 * 128
        part = fac_t.at[rows(q), pl.ds(first, n - first)]
        return copy(part, part, g_send.at[0, i], g_recv.at[0, i], t, to)

    def for_chip(dx, action):
        for xs in range(chips):
            cond = lambda xs=xs: lax.rem(x + chips + dx, chips) == xs
            pl.when(cond())(lambda xs=xs, cond=cond: action(xs, cond))

    def start_triangle():
        def sends(xs, cond):
            for dx in (2, 1, 3):
                send(cond, lambda dx=dx: triangle_copy(xs, p, dx - 1, away(dx, c)))
            send(cond, lambda: triangle_copy(xs, p, 3, sibling))

        for_chip(0, sends)

    def finish_triangle():
        def forward(dx, xs, cond):
            triangle_copy(xs, away(-dx, c), dx - 1, sibling).wait_recv()
            send(cond, lambda: triangle_copy(xs, away(-dx, c), 3 + dx, sibling))

        for dx in (1, 3, 2):
            for_chip(-dx, functools.partial(forward, dx))
        for_chip(0, lambda xs, cond: triangle_copy(xs, sibling, 3, sibling).wait_recv())
        for dx in (1, 3, 2):
            for_chip(-dx, lambda xs, cond, dx=dx: triangle_copy(xs, away(-dx, 1 - c), 3 + dx, sibling).wait_recv())

    def exchange_copy(k, src, dst, j, to):
        return copy(blocks.at[k, src], gathered.at[k, rows(dst)], a_send.at[k, j - 1], a_recv.at[k, j - 1], t, to)

    def put_blocks(k, panel):
        wide = jnp.concatenate([panel, panel[:, :128]], axis=1)
        for q in range(panels):
            blocks[k, q] = wide[:, q * width : q * width + 128]

    def send_blocks(k, cond=None):
        for j in sorted(range(1, panels), key=lambda j: abs(j - chips)):
            q = lambda j=j: lax.rem(p + j, panels)
            send(cond, lambda j=j, q=q: exchange_copy(k, q(), p, j, q()))
        gathered[k, rows(p)] = blocks[k, p]

    def start_exchange(k, panel, cond=None):
        put_blocks(k, panel)
        send_blocks(k, cond)

    def finish_exchange(k):
        for j in range(1, panels):
            q = lax.rem(p + panels - j, panels)
            exchange_copy(k, q, q, j, q).wait_recv()

    def comp_copy(r, to):
        return copy(comp.at[r, rows(p)], comp_recv.at[r], t_send.at[r, 0], t_recv.at[r, 0], to, p)

    def cov_copy(r, to):
        return copy(cov_send.at[r], cov_recv.at[r], t_send.at[r, 1], t_recv.at[r, 1], to, p)

    def send_comp(r):
        @pl.when(has_target(r))
        def _():
            send(target[r], lambda: comp_copy(r, t - (1 << r)))

    def send_cov(r):
        cov_send[r] = own_cov[...].astype(BF16)

        @pl.when(has_target(r))
        def _():
            send(target[r], lambda: cov_copy(r, t - (1 << r)))

    loads = [
        pltpu.make_async_copy(coupling_ref, coupling_buf, load_sem.at[0]),
        pltpu.make_async_copy(factor_ref, factor_buf, load_sem.at[1]),
    ]
    for load in loads:
        load.start()

    @pl.when(last)
    def _():
        pltpu.make_async_copy(sigma_ref, sigma_buf, load_sem.at[2]).start()

    fac_t[...] = jnp.zeros_like(fac_t)
    barrier = pltpu.get_barrier_semaphore()
    for j in range(1, panels):
        pl.semaphore_signal(barrier, 1, device_id=(t, lax.rem(p + j, panels)), device_id_type=MESH)
    for r in range(rounds):
        @pl.when(has_target(r))
        def _():
            pl.semaphore_signal(barrier, 1, device_id=(t - (1 << r), p), device_id_type=MESH)

        @pl.when(has_source(r))
        def _():
            pl.semaphore_signal(barrier, 1, device_id=(t + (1 << r), p), device_id_type=MESH)

    loads[0].wait()
    comp_t[rows(p)] = coupling_buf[...].astype(BF16)
    loads[1].wait()
    fac_high, fac_low = split(factor_buf[...])
    fac_t[rows(p)] = fac_high

    peers = panels - 1
    for r in range(rounds):
        peers += has_target(r).astype(jnp.int32) + has_source(r).astype(jnp.int32)
    pl.semaphore_wait(barrier, peers)

    start_gather(rounds, lambda: comp_t)
    start_triangle()
    near_gather(rounds, lambda: comp_t)
    finish_gather(rounds, lambda: comp_t)
    for j in range(n // 128):
        comp[0, :, 128 * j : 128 * (j + 1)] = comp_t[128 * j : 128 * (j + 1), :].T
    send_comp(0)
    finish_triangle()
    both = dot_nt(jnp.concatenate([fac_high, fac_low]), fac_t[...])
    own_cov[...] = both[:width] + both[width:]

    @pl.when(last)
    def _():
        pltpu.make_async_copy(sigma_ref, sigma_buf, load_sem.at[2]).wait()
        sig_high, sig_low = split(sigma_buf[...])
        own = comp_t[rows(p)]
        w_high, w_low = split(dot(own, sig_high) + dot(own, sig_low))
        own_cov[...] += dot(w_high, comp[0]) + dot(w_low, comp[0])

    send_cov(0)

    for r in range(rounds):
        active = has_source(r)
        more = r + 1 < rounds
        old = pending[:-1]
        if r:
            @pl.when(active)
            def _():
                finish_gather(r, lambda r=r: comp.at[r], source[r])

        @pl.when(active)
        def _():
            comp_copy(r, t).wait_recv()
            panel = dot(comp_recv[r], comp[r]).astype(BF16)
            if more:
                comp[r + 1, rows(p)] = panel
            else:
                put_blocks(rounds, panel)

        @pl.when(jnp.logical_not(active))
        def _():
            if more:
                comp[r + 1, rows(p)] = comp[r, rows(p)]
            else:
                put_blocks(rounds, comp[r, rows(p)])

        if more:
            send_comp(r + 1)

            @pl.when(has_source(r + 1))
            def _():
                start_gather(r + 1, lambda r=r: comp.at[r + 1], source[r + 1])
        else:
            send_blocks(rounds)

        drain(old)

        @pl.when(active)
        def _():
            cov_copy(r, t).wait_recv()
            start_exchange(r, dot(cov_recv[r], comp[r]).astype(BF16), source[r])

        if more:
            @pl.when(has_source(r + 1))
            def _():
                near_gather(r + 1, lambda r=r: comp.at[r + 1], source[r + 1])

        if not more:
            finish_exchange(rounds)
            prop_out[...] = gathered[rounds].T[:width]

        @pl.when(active)
        def _():
            finish_exchange(r)
            own_cov[...] += dot(gathered[r].T[:width], comp[r])

        if more:
            send_cov(r + 1)

    cov_out[...] = own_cov[...]
    drain(pending[:])


def shards(factor_inverse, coupling, sigma_after):
    steps, panels = lax.axis_size("tm"), lax.axis_size("panel")
    n, width = factor_inverse.shape[1:]
    rounds = (steps - 1).bit_length()
    chips = panels // 2
    vmem = pl.BlockSpec(memory_space=pltpu.VMEM)
    cov, prop = pl.pallas_call(
        functools.partial(kernel, steps, chips, rounds),
        out_shape=(
            jax.ShapeDtypeStruct((width, n), F32),
            jax.ShapeDtypeStruct((width, n), BF16),
        ),
        in_specs=[pl.BlockSpec(memory_space=pl.ANY)] * 3,
        out_specs=(vmem, vmem),
        scratch_shapes=[
            pltpu.VMEM((rounds, n, n), BF16),
            pltpu.VMEM((n, n), BF16),
            pltpu.VMEM((n, n), BF16),
            pltpu.VMEM((width, n), F32),
            pltpu.VMEM((width, n), F32),
            pltpu.VMEM((width, n), F32),
            pltpu.VMEM((rounds, width, n), BF16),
            pltpu.VMEM((rounds, width, n), BF16),
            pltpu.VMEM((rounds, width, n), BF16),
            pltpu.VMEM((rounds + 1, panels, width, 128), BF16),
            pltpu.VMEM((rounds + 1, n, 128), BF16),
            pltpu.VMEM((n, n), F32),
            pltpu.SemaphoreType.DMA((rounds + 1, 7)),
            pltpu.SemaphoreType.DMA((rounds + 1, 7)),
            pltpu.SemaphoreType.DMA((rounds, 2)),
            pltpu.SemaphoreType.DMA((rounds, 2)),
            pltpu.SemaphoreType.DMA((rounds + 1, panels - 1)),
            pltpu.SemaphoreType.DMA((rounds + 1, panels - 1)),
            pltpu.SemaphoreType.DMA((3,)),
        ],
        compiler_params=pltpu.CompilerParams(
            collective_id=0, has_side_effects=True, vmem_limit_bytes=55_990_000
        ),
        name="scan",
    )(factor_inverse[0].T, coupling[0].T, sigma_after)
    return cov.T[None], prop.T[None]


def solution(mesh):
    placed = (P("tm", None, "panel"), P("tm", None, "panel"), P())
    return jax.shard_map(
        shards,
        mesh=mesh,
        in_specs=placed,
        out_specs=(P("tm", None, "panel"), P("tm", None, "panel")),
        check_vma=False,
    )
```

```python
import functools

import jax
import jax.numpy as jnp
from jax import lax
from jax.experimental import pallas as pl
from jax.experimental.pallas import tpu as pltpu
from jax.sharding import PartitionSpec as P

MESH = pl.DeviceIdType.MESH
F32 = jnp.float32
BF16 = jnp.bfloat16


def dot(a, b):
    return jnp.dot(a, b, preferred_element_type=F32)


def dot_nt(a, b):
    return lax.dot_general(a, b, (((1,), (1,)), ((), ())), preferred_element_type=F32)


def split(a):
    high = a.astype(BF16)
    return high, (a - high.astype(F32)).astype(BF16)


def kernel(
    steps, chips, rounds,
    factor_ref, coupling_ref, sigma_ref, cov_out, prop_out,
    comp, comp_t, fac_t, coupling_buf, factor_buf, own_cov, cov_send, comp_recv, cov_recv, blocks, gathered, sigma_buf,
    g_send, g_recv, t_send, t_recv, a_send, a_recv, load_sem,
):
    width, n = own_cov.shape
    panels = 2 * chips
    t = lax.axis_index("tm")
    p = lax.axis_index("panel")
    x, c = lax.div(p, 2), lax.rem(p, 2)
    sibling = 2 * x + 1 - c
    last = t == steps - 1
    pending = []

    def has_source(r):
        return t + (1 << r) < steps

    def has_target(r):
        return t - (1 << r) >= 0

    def rows(q):
        return pl.ds(pl.multiple_of(q * width, 32), width)

    def away(dx, core):
        return 2 * lax.rem(x + chips + dx, chips) + core

    def send(cond, make):
        make().start()
        pending.append((cond, make))

    def copy(src, dst, s, r, tm, panel):
        return pltpu.make_async_remote_copy(
            src_ref=src, dst_ref=dst, send_sem=s, recv_sem=r, device_id=(tm, panel), device_id_type=MESH
        )

    def drain(sent):
        groups = {}
        for entry in sent:
            pending.remove(entry)
            groups.setdefault(entry[0], []).append(entry[1])
        for cond, makes in groups.items():
            def waits(makes=makes):
                for make in makes:
                    make().wait_send()

            waits() if cond is None else pl.when(cond())(waits)

    source = [lambda r=r: has_source(r) for r in range(rounds)]
    target = [lambda r=r: has_target(r) for r in range(rounds)]

    def gather_copy(k, buf, q, i, to):
        return copy(buf().at[rows(q)], buf().at[rows(q)], g_send.at[k, i], g_recv.at[k, i], t, to)

    def start_gather(k, buf, cond=None, direct=False):
        if direct:
            for dx in (2, 1, 3):
                send(cond, lambda dx=dx: gather_copy(k, buf, p, dx - 1, away(dx, c)))
        else:
            for side in (1, -1):
                way = lambda side=side: side * (1 - 2 * c)
                send(cond, lambda way=way: gather_copy(k, buf, p, 1 - way(), away(way(), c)))
        send(cond, lambda: gather_copy(k, buf, p, 3, sibling))

    def near_gather(k, buf, cond=None):
        for side in (1, -1):
            q = lambda side=side: away(side * (2 * c - 1), c)
            i = lambda side=side: 1 + side * (2 * c - 1)
            gather_copy(k, buf, q(), i(), sibling).wait_recv()
            if side == 1:
                send(cond, lambda q=q: gather_copy(k, buf, q(), 1, away(1 - 2 * c, c)))
            send(cond, lambda q=q, i=i: gather_copy(k, buf, q(), 4 + i(), sibling))

    def finish_gather(k, buf, cond=None, order=(2,)):
        for dx in order:
            gather_copy(k, buf, away(-dx, c), dx - 1, sibling).wait_recv()
            send(cond, lambda dx=dx: gather_copy(k, buf, away(-dx, c), 3 + dx, sibling))
        gather_copy(k, buf, sibling, 3, sibling).wait_recv()
        for dx in (1, 3, 2)[: chips - 1] if chips > 2 else (1,):
            gather_copy(k, buf, away(-dx, 1 - c), 3 + dx, sibling).wait_recv()

    def triangle_copy(xs, q, i, to):
        first = 2 * width * xs // 128 * 128
        part = fac_t.at[rows(q), pl.ds(first, n - first)]
        return copy(part, part, g_send.at[0, i], g_recv.at[0, i], t, to)

    def for_chip(dx, action):
        for xs in range(chips):
            cond = lambda xs=xs: lax.rem(x + chips + dx, chips) == xs
            pl.when(cond())(lambda xs=xs, cond=cond: action(xs, cond))

    def start_triangle():
        def sends(xs, cond):
            for dx in (2, 1, 3):
                send(cond, lambda dx=dx: triangle_copy(xs, p, dx - 1, away(dx, c)))
            send(cond, lambda: triangle_copy(xs, p, 3, sibling))

        for_chip(0, sends)

    def finish_triangle():
        def forward(dx, xs, cond):
            triangle_copy(xs, away(-dx, c), dx - 1, sibling).wait_recv()
            send(cond, lambda: triangle_copy(xs, away(-dx, c), 3 + dx, sibling))

        for dx in (1, 3, 2):
            for_chip(-dx, functools.partial(forward, dx))
        for_chip(0, lambda xs, cond: triangle_copy(xs, sibling, 3, sibling).wait_recv())
        for dx in (1, 3, 2):
            for_chip(-dx, lambda xs, cond, dx=dx: triangle_copy(xs, away(-dx, 1 - c), 3 + dx, sibling).wait_recv())

    def exchange_copy(k, src, dst, j, to):
        return copy(blocks.at[k, src], gathered.at[k, rows(dst)], a_send.at[k, j - 1], a_recv.at[k, j - 1], t, to)

    def put_blocks(k, panel):
        wide = jnp.concatenate([panel, panel[:, :128]], axis=1)
        for q in range(panels):
            blocks[k, q] = wide[:, q * width : q * width + 128]

    def send_blocks(k, cond=None):
        for j in sorted(range(1, panels), key=lambda j: abs(j - chips)):
            q = lambda j=j: lax.rem(p + j, panels)
            send(cond, lambda j=j, q=q: exchange_copy(k, q(), p, j, q()))
        gathered[k, rows(p)] = blocks[k, p]

    def start_exchange(k, panel, cond=None):
        put_blocks(k, panel)
        send_blocks(k, cond)

    def finish_exchange(k):
        for j in range(1, panels):
            q = lax.rem(p + panels - j, panels)
            exchange_copy(k, q, q, j, q).wait_recv()

    def comp_copy(r, to):
        return copy(comp.at[r, rows(p)], comp_recv.at[r], t_send.at[r, 0], t_recv.at[r, 0], to, p)

    def cov_copy(r, to):
        return copy(cov_send.at[r], cov_recv.at[r], t_send.at[r, 1], t_recv.at[r, 1], to, p)

    def send_comp(r):
        @pl.when(has_target(r))
        def _():
            send(target[r], lambda: comp_copy(r, t - (1 << r)))

    def send_cov(r):
        cov_send[r] = own_cov[...].astype(BF16)

        @pl.when(has_target(r))
        def _():
            send(target[r], lambda: cov_copy(r, t - (1 << r)))

    loads = [
        pltpu.make_async_copy(coupling_ref, coupling_buf, load_sem.at[0]),
        pltpu.make_async_copy(factor_ref, factor_buf, load_sem.at[1]),
    ]
    for load in loads:
        load.start()

    @pl.when(last)
    def _():
        pltpu.make_async_copy(sigma_ref, sigma_buf, load_sem.at[2]).start()

    fac_t[...] = jnp.zeros_like(fac_t)
    barrier = pltpu.get_barrier_semaphore()
    for j in range(1, panels):
        pl.semaphore_signal(barrier, 1, device_id=(t, lax.rem(p + j, panels)), device_id_type=MESH)
    for r in range(rounds):
        @pl.when(has_target(r))
        def _():
            pl.semaphore_signal(barrier, 1, device_id=(t - (1 << r), p), device_id_type=MESH)

        @pl.when(has_source(r))
        def _():
            pl.semaphore_signal(barrier, 1, device_id=(t + (1 << r), p), device_id_type=MESH)

    loads[0].wait()
    comp_t[rows(p)] = coupling_buf[...].astype(BF16)
    loads[1].wait()
    fac_high, fac_low = split(factor_buf[...])
    fac_t[rows(p)] = fac_high

    peers = panels - 1
    for r in range(rounds):
        peers += has_target(r).astype(jnp.int32) + has_source(r).astype(jnp.int32)
    pl.semaphore_wait(barrier, peers)

    start_gather(rounds, lambda: comp_t, None, True)
    start_triangle()
    finish_gather(rounds, lambda: comp_t, None, (1, 3, 2))
    for j in range(n // 128):
        comp[0, :, 128 * j : 128 * (j + 1)] = comp_t[128 * j : 128 * (j + 1), :].T
    send_comp(0)
    finish_triangle()
    both = dot_nt(jnp.concatenate([fac_high, fac_low]), fac_t[...])
    own_cov[...] = both[:width] + both[width:]

    @pl.when(last)
    def _():
        pltpu.make_async_copy(sigma_ref, sigma_buf, load_sem.at[2]).wait()
        sig_high, sig_low = split(sigma_buf[...])
        own = comp_t[rows(p)]
        w_high, w_low = split(dot(own, sig_high) + dot(own, sig_low))
        own_cov[...] += dot(w_high, comp[0]) + dot(w_low, comp[0])

    send_cov(0)

    for r in range(rounds):
        active = has_source(r)
        more = r + 1 < rounds
        old = pending[:-1]
        if r:
            @pl.when(active)
            def _():
                finish_gather(r, lambda r=r: comp.at[r], source[r])

        @pl.when(active)
        def _():
            comp_copy(r, t).wait_recv()
            panel = dot(comp_recv[r], comp[r]).astype(BF16)
            if more:
                comp[r + 1, rows(p)] = panel
            else:
                put_blocks(rounds, panel)

        @pl.when(jnp.logical_not(active))
        def _():
            if more:
                comp[r + 1, rows(p)] = comp[r, rows(p)]
            else:
                put_blocks(rounds, comp[r, rows(p)])

        if more:
            send_comp(r + 1)

            @pl.when(has_source(r + 1))
            def _():
                start_gather(r + 1, lambda r=r: comp.at[r + 1], source[r + 1])
        else:
            send_blocks(rounds)

        drain(old)

        @pl.when(active)
        def _():
            cov_copy(r, t).wait_recv()
            start_exchange(r, dot(cov_recv[r], comp[r]).astype(BF16), source[r])

        if more:
            @pl.when(has_source(r + 1))
            def _():
                near_gather(r + 1, lambda r=r: comp.at[r + 1], source[r + 1])

        if not more:
            finish_exchange(rounds)
            prop_out[...] = gathered[rounds].T[:width]

        @pl.when(active)
        def _():
            finish_exchange(r)
            own_cov[...] += dot(gathered[r].T[:width], comp[r])

        if more:
            send_cov(r + 1)

    cov_out[...] = own_cov[...]
    drain(pending[:])


def shards(factor_inverse, coupling, sigma_after):
    steps, panels = lax.axis_size("tm"), lax.axis_size("panel")
    n, width = factor_inverse.shape[1:]
    rounds = (steps - 1).bit_length()
    chips = panels // 2
    vmem = pl.BlockSpec(memory_space=pltpu.VMEM)
    cov, prop = pl.pallas_call(
        functools.partial(kernel, steps, chips, rounds),
        out_shape=(
            jax.ShapeDtypeStruct((width, n), F32),
            jax.ShapeDtypeStruct((width, n), BF16),
        ),
        in_specs=[pl.BlockSpec(memory_space=pl.ANY)] * 3,
        out_specs=(vmem, vmem),
        scratch_shapes=[
            pltpu.VMEM((rounds, n, n), BF16),
            pltpu.VMEM((n, n), BF16),
            pltpu.VMEM((n, n), BF16),
            pltpu.VMEM((width, n), F32),
            pltpu.VMEM((width, n), F32),
            pltpu.VMEM((width, n), F32),
            pltpu.VMEM((rounds, width, n), BF16),
            pltpu.VMEM((rounds, width, n), BF16),
            pltpu.VMEM((rounds, width, n), BF16),
            pltpu.VMEM((rounds + 1, panels, width, 128), BF16),
            pltpu.VMEM((rounds + 1, n, 128), BF16),
            pltpu.VMEM((n, n), F32),
            pltpu.SemaphoreType.DMA((rounds + 1, 7)),
            pltpu.SemaphoreType.DMA((rounds + 1, 7)),
            pltpu.SemaphoreType.DMA((rounds, 2)),
            pltpu.SemaphoreType.DMA((rounds, 2)),
            pltpu.SemaphoreType.DMA((rounds + 1, panels - 1)),
            pltpu.SemaphoreType.DMA((rounds + 1, panels - 1)),
            pltpu.SemaphoreType.DMA((3,)),
        ],
        compiler_params=pltpu.CompilerParams(
            collective_id=0, has_side_effects=True, vmem_limit_bytes=55_990_000
        ),
        name="scan",
    )(factor_inverse[0].T, coupling[0].T, sigma_after)
    return cov.T[None], prop.T[None]


def solution(mesh):
    placed = (P("tm", None, "panel"), P("tm", None, "panel"), P())
    return jax.shard_map(
        shards,
        mesh=mesh,
        in_specs=placed,
        out_specs=(P("tm", None, "panel"), P("tm", None, "panel")),
        check_vma=False,
    )
```
